128 devices in a mesh: trainer: 4 (over x_lo, core), encode: 32 (over x_hi, z, y).
Axes of the slice: x: 4 (x_hi: 2, x_lo: 2; x = x_hi * 2 + x_lo), y: 4, z: 4, core: 2. Of those that a mesh axis runs over, the one named last changes fastest.
Arguments:
- hidden_in: bfloat16 [32768, 1024], P('encode'), may hold values from -8 to 8
- token_ids: int32 [32768], P('encode'), may hold values from 0 to 30521
- lengths: int32 [64, 8], P('encode'), may hold values from 0 to 448, as said below
- owners: int32 [64, 8], P('encode'), may hold values from 0 to 31, as said below
- w_query: bfloat16 [2, 1024, 1024], P(None, 'encode', 'trainer'), may hold values from -6 to 6
- w_key: bfloat16 [2, 1024, 1024], P(None, 'encode', 'trainer'), may hold values from -6 to 6
- w_value: bfloat16 [2, 1024, 1024], P(None, 'encode', 'trainer'), may hold values from -0.1875 to 0.1875
- w_out: bfloat16 [2, 1024, 1024], P(None, 'trainer', 'encode'), may hold values from -0.1875 to 0.1875
- w_up: bfloat16 [2, 1024, 4096], P(None, 'encode', 'trainer'), may hold values from -0.1875 to 0.1875
- w_down: bfloat16 [2, 4096, 1024], P(None, 'trainer', 'encode'), may hold values from -0.09375 to 0.09375
- gains: float32 [2, 2, 1024], replicated, may hold values from 0.5 to 1.5
Outputs:
- index_rows: bfloat16 [32, 32, 2, 1024], P('encode', None, None, 'trainer')
The draws below stay inside these ranges and needn't reach their ends.
Inputs may be any that keep to these rules, and one draw needn't show every extreme that they name: `lengths`: each row is one bin: first its live passages in token order, each of 64 or more tokens, then zeros; every row sums to 512 and holds at least two live passages. `owners`: read only where the length is nonzero. Within one source block at most 2 live passages share an owner, and one owner takes exactly 2 live passages from every source block.
All inputs are finite; a program needn't handle non-finite values.
Results may differ from the reference program's by a relative error of at most 0.029.
Values may be sent and summed in bfloat16 or wider, within the bound.
No kernel may reach another device: no remote copies, remote signals or barrier semaphores. Data moves between devices by JAX's collectives and lax.ppermute only.
A program may use at most 128 MiB of HBM per device.

```python
import jax
import jax.numpy as jnp
from jax import lax

D = 1024
HEADS = 16
FF = 4096
VOCAB = 30522
HEAD_DIM = 64
LAYERS = 2
BIN = 512
MIN_LEN = 64
SKIP_IDS = 2000
TOKENS = 32768
BINS = 64
PER_BIN = 8
SLOTS_DEV = 16
CAP = 2
N_TRAINER = 4
N_ENCODE = 32


def packing_plan(key):
    plan_key = jax.random.fold_in(key, 101)
    count_key, special_key, cut_key = jax.random.split(plan_key, 3)
    bin_index = jnp.arange(BINS, dtype=jnp.int32)
    counts = jax.random.randint(count_key, (BINS,), 2, PER_BIN + 1).astype(jnp.int32)
    special = jax.random.randint(special_key, (), 0, BINS).astype(jnp.int32)
    counts = jnp.where(bin_index == special, 2, counts)
    spare = (BIN - MIN_LEN * counts).astype(jnp.int32)
    cuts = jax.random.randint(cut_key, (BINS, PER_BIN - 1), 0, spare[:, None] + 1).astype(jnp.int32)
    cut_index = jnp.arange(PER_BIN - 1, dtype=jnp.int32)
    cuts = jnp.where(cut_index[None, :] < counts[:, None] - 1, cuts, spare[:, None])
    forced = jnp.where(cut_index[None, :] < 1, 0, spare[:, None])
    cuts = jnp.where((bin_index == special)[:, None], forced, cuts)
    cuts = jnp.sort(cuts, axis=1)
    bounds = jnp.concatenate([jnp.zeros((BINS, 1), jnp.int32), cuts, spare[:, None]], axis=1)
    extra = bounds[:, 1:] - bounds[:, :-1]
    slot_index = jnp.arange(PER_BIN, dtype=jnp.int32)
    return jnp.where(slot_index[None, :] < counts[:, None], MIN_LEN + extra, 0).astype(jnp.int32)


def query_matrix(key):
    return jax.random.normal(jax.random.fold_in(key, 211), (LAYERS, D, D), jnp.float32) * D ** (-0.5)


def draw_lengths(key, part):
    return packing_plan(key)


def draw_owners(key, part):
    lengths = packing_plan(key)
    key = jax.random.fold_in(key, 2)
    hot_key, score_key, order_key, unused_key = jax.random.split(key, 4)
    live = (lengths > 0).reshape(N_ENCODE, SLOTS_DEV)
    slot_index = jnp.arange(SLOTS_DEV, dtype=jnp.int32)
    hot = jax.random.randint(hot_key, (), 0, N_ENCODE).astype(jnp.int32)
    scores = jax.random.randint(score_key, (N_ENCODE, SLOTS_DEV), 0, 1 << 20).astype(jnp.int32) * SLOTS_DEV + slot_index[None, :]
    scores = jnp.where(live, scores, (1 << 20) * SLOTS_DEV + slot_index[None, :])
    position = jnp.argsort(jnp.argsort(scores, axis=1), axis=1)
    chosen = live & (position < CAP)
    rest = live & jnp.logical_not(chosen)
    turn = jnp.cumsum(rest.astype(jnp.int32), axis=1) - 1
    others = N_ENCODE - 1
    other_index = jnp.arange(others, dtype=jnp.int32)
    shuffle_scores = jax.random.randint(order_key, (N_ENCODE, others), 0, 1 << 20).astype(jnp.int32) * others + other_index[None, :]
    shuffle = jnp.argsort(shuffle_scores, axis=1).astype(jnp.int32)
    pick = jnp.take_along_axis(shuffle, jnp.mod(jnp.maximum(turn, 0), others), axis=1).astype(jnp.int32)
    pick = pick + (pick >= hot).astype(jnp.int32)
    unused = jax.random.randint(unused_key, (N_ENCODE, SLOTS_DEV), 0, N_ENCODE).astype(jnp.int32)
    result = jnp.where(chosen, hot, jnp.where(rest, pick, unused))
    return result.reshape(BINS, PER_BIN).astype(jnp.int32)


def draw_token_ids(key, part):
    key = jax.random.fold_in(key, 3)
    pick_key, low_key, high_key = jax.random.split(key, 3)
    pick = jax.random.randint(pick_key, (TOKENS,), 0, 4)
    low = jax.random.randint(low_key, (TOKENS,), 0, SKIP_IDS)
    high = jax.random.randint(high_key, (TOKENS,), SKIP_IDS, VOCAB)
    return jnp.where(pick == 0, low, high).astype(jnp.int32)


def draw_w_query(key, part):
    return query_matrix(key).astype(jnp.bfloat16)


def draw_w_key(key, part):
    key = jax.random.fold_in(key, 5)
    own_key = jax.random.fold_in(key, 0)
    own = jax.random.normal(own_key, (LAYERS, D, D), jnp.float32) * D ** (-0.5)
    return own.astype(jnp.bfloat16)


def draw_hidden_in(key, part):
    key = jax.random.fold_in(key, 6)
    base_key = jax.random.fold_in(key, 0)
    return jnp.clip(jax.random.normal(base_key, (TOKENS, D), jnp.float32), -6.0, 6.0).astype(jnp.bfloat16)


def block_levels(rng, dims, cuts, smallest, largest):
    level = 1.0
    for dim, parts in cuts:
        heights = jax.random.uniform(jax.random.fold_in(jax.random.fold_in(rng, 6), dim), (parts,), jnp.float32, smallest / len(cuts), largest / len(cuts))
        level = level * jnp.repeat(jnp.exp(heights), dims[dim] // parts).reshape((-1,) + (1,) * (len(dims) - 1 - dim))
    return level


def bell_draw(key, dims, deviation, reach, cuts=(), kind=jnp.bfloat16):
    level = block_levels(key, dims, cuts, -0.22, 0.18) if cuts else 1.0
    values = jax.random.normal(key, dims, jnp.float32) * deviation * level
    return jnp.minimum(jnp.maximum(values, -reach), reach).astype(kind)


def setup_inputs(seed: int = 0) -> dict:
    splits = jax.random.split(jax.random.key(seed), 12)
    hidden_in = draw_hidden_in(jax.random.fold_in(splits[11], 71), 0)
    token_ids = draw_token_ids(jax.random.fold_in(splits[11], 71), 0)
    lengths = draw_lengths(jax.random.fold_in(splits[11], 71), 0)
    owners = draw_owners(jax.random.fold_in(splits[11], 71), 0)
    w_query = draw_w_query(jax.random.fold_in(splits[11], 71), 0)
    w_key = draw_w_key(jax.random.fold_in(splits[11], 71), 0)
    w_value = bell_draw(splits[6], (LAYERS, D, D), D ** -0.5, 0.1875, ((1, 32), (2, 4)))
    w_out = bell_draw(splits[7], (LAYERS, D, D), D ** -0.5, 0.1875, ((1, 4), (2, 32)))
    w_up = bell_draw(splits[8], (LAYERS, D, FF), D ** -0.5, 0.1875, ((1, 32), (2, 4)))
    w_down = bell_draw(splits[9], (LAYERS, FF, D), FF ** -0.5, 0.09375, ((1, 4), (2, 32)))
    gains = jnp.clip(1.0 + 0.1 * jax.random.normal(splits[10], (LAYERS, 2, D), jnp.float32), 0.5, 1.5)
    return {"hidden_in": hidden_in, "token_ids": token_ids, "lengths": lengths, "owners": owners, "w_query": w_query, "w_key": w_key, "w_value": w_value, "w_out": w_out, "w_up": w_up, "w_down": w_down, "gains": gains}


EPSILON = 1e-05

def rounded(values):
    return lax.optimization_barrier(values.astype(jnp.bfloat16))

def normalize(values, gain):
    mean = lax.optimization_barrier(jnp.mean(values, axis=-1, keepdims=True))
    centered = values - mean
    spread = lax.optimization_barrier(jnp.mean(centered * centered, axis=-1, keepdims=True))
    return centered * lax.rsqrt(spread + EPSILON) * gain

def passage_tables(lengths):
    ends = jnp.cumsum(lengths, axis=1)
    starts = ends - lengths
    place = jnp.arange(BIN, dtype=jnp.int32)
    segment = lax.optimization_barrier(jnp.sum((place[None, :, None] >= ends[:, None, :]).astype(jnp.int32), axis=2))
    opening = jnp.any((place[None, :, None] == starts[:, None, :]) & (lengths[:, None, :] > 0), axis=2)
    return (segment, opening)

def attention(query, keys, values, segment):
    shape = (BIN, HEADS, HEAD_DIM)

    def one_bin(inputs):
        block_query, block_keys, block_values, block_segment = inputs
        scores = jnp.einsum('qhd,khd->hqk', block_query.reshape(shape).astype(jnp.float32), block_keys.reshape(shape).astype(jnp.float32), precision=lax.Precision.HIGHEST) * HEAD_DIM ** (-0.5)
        same = block_segment[None, :, None] == block_segment[None, None, :]
        scores = jnp.where(same, scores, -1e+30)
        highest = lax.optimization_barrier(jnp.max(scores, axis=-1, keepdims=True))
        weights = jnp.exp(scores - highest)
        probs = rounded(weights / lax.optimization_barrier(jnp.sum(weights, axis=-1, keepdims=True)))
        context = jnp.einsum('hqk,khd->qhd', probs.astype(jnp.float32), block_values.reshape(shape).astype(jnp.float32), precision=lax.Precision.HIGHEST)
        return rounded(context).reshape(BIN, D)
    result = lax.map(one_bin, (query.reshape(BINS, BIN, D), keys.reshape(BINS, BIN, D), values.reshape(BINS, BIN, D), segment))
    return result.reshape(TOKENS, D)

def split_sum(left, right, width):
    total = jnp.zeros((left.shape[0], right.shape[1]), jnp.float32)
    for part_index in range(N_TRAINER):
        term = jnp.dot(left[:, part_index * width:(part_index + 1) * width], right[part_index * width:(part_index + 1) * width], preferred_element_type=jnp.float32)
        total = total + rounded(term).astype(jnp.float32)
    return total

def reference(hidden_in, token_ids, lengths, owners, w_query, w_key, w_value, w_out, w_up, w_down, gains):
    segment, opening = passage_tables(lengths)
    hidden = hidden_in
    for layer_index in range(LAYERS):
        query = rounded(jnp.dot(hidden, w_query[layer_index], preferred_element_type=jnp.float32))
        keys = rounded(jnp.dot(hidden, w_key[layer_index], preferred_element_type=jnp.float32))
        values = rounded(jnp.dot(hidden, w_value[layer_index], preferred_element_type=jnp.float32))
        context = attention(query, keys, values, segment)
        attn_sum = split_sum(context, w_out[layer_index], D // N_TRAINER)
        mixed = rounded(normalize(hidden.astype(jnp.float32) + attn_sum, gains[layer_index, 0]))
        raised = jnp.dot(mixed, w_up[layer_index], preferred_element_type=jnp.float32)
        activated = rounded(jax.nn.gelu(raised, approximate=False))
        ffn_sum = split_sum(activated, w_down[layer_index], FF // N_TRAINER)
        hidden = rounded(normalize(mixed.astype(jnp.float32) + ffn_sum, gains[layer_index, 1]))
    keep = (token_ids.reshape(BINS, BIN) >= SKIP_IDS) | opening
    member = ((segment[:, None, :] == jnp.arange(PER_BIN, dtype=jnp.int32)[None, :, None]) & keep[:, None, :]).astype(jnp.float32)
    sums = jnp.einsum('bjt,btd->bjd', member, hidden.reshape(BINS, BIN, D).astype(jnp.float32), precision=lax.Precision.HIGHEST)
    counts = lax.optimization_barrier(jnp.sum(member, axis=2))
    safe_counts = jnp.where(counts > 0, counts, 1.0)
    pooled = rounded(sums / safe_counts[:, :, None]).reshape(N_ENCODE, SLOTS_DEV, D)
    live = (lengths > 0).reshape(N_ENCODE, SLOTS_DEV)
    target_owner = owners.reshape(N_ENCODE, SLOTS_DEV)
    order = jnp.arange(SLOTS_DEV, dtype=jnp.int32)
    earlier = (target_owner[:, None, :] == target_owner[:, :, None]) & live[:, None, :] & (order[None, None, :] < order[None, :, None])
    rank = lax.optimization_barrier(jnp.sum(earlier.astype(jnp.int32), axis=2))
    target = target_owner * CAP + rank
    placing = ((jnp.arange(N_ENCODE * CAP, dtype=jnp.int32)[None, :, None] == target[:, None, :]) & live[:, None, :]).astype(jnp.float32)
    outgoing = jnp.einsum('sop,spd->sod', placing, pooled.astype(jnp.float32), precision=lax.Precision.HIGHEST)
    outgoing = outgoing.astype(jnp.bfloat16).reshape(N_ENCODE, N_ENCODE, CAP, D)
    return jnp.transpose(outgoing, (1, 0, 2, 3))
```

```python
import functools

import jax
import jax.numpy as jnp
from jax import lax
from jax.experimental import pallas as pl
from jax.experimental.pallas import tpu as pltpu
from jax.sharding import Mesh, PartitionSpec as P

SKIP_IDS = 2000
EPSILON = 1e-05
LOG2E = 1.4426950408889634
HEAD = 64
BIN = 512
D = 1024
RING = 4
NT = (((1,), (1,)), ((), ()))


def x_line(x, core):
    return ((x % 2) * 2 + core) * 2 + x // 2


def hop(value, axis):
    pairs = []
    for core in range(2):
        step = 1 if core == 0 else -1
        for at in range(RING):
            to = (at + step) % RING
            if axis == "x":
                pairs.append((x_line(at, core), x_line(to, core)))
            else:
                pairs.append((core * RING + at, core * RING + to))
    names = ("x_lo", "core", "x_hi") if axis == "x" else ("core", axis)
    return lax.ppermute(value, names, pairs)


def shift(value, axis, by):
    if axis == "x":
        line = [(at % 2) * 2 + at // 2 for at in range(RING)]
        pairs = [(line[at], line[(at + by) % RING]) for at in range(RING)]
        return lax.ppermute(value, ("x_lo", "x_hi"), pairs)
    return lax.ppermute(value, axis, [(at, (at + by) % RING) for at in range(RING)])


def swap(value):
    return lax.ppermute(value, "core", [(0, 1), (1, 0)])


def ring(value, axis):
    blocks = [value]
    for _ in range(RING - 1):
        blocks.append(hop(blocks[-1], axis))
    return blocks


def spread(shard, order):
    first = ring(shard[None], order[0])
    second = ring(jnp.concatenate(first, axis=0), order[1])
    return ring(jnp.concatenate(second, axis=0), order[2])


def block_table(order, place, core):
    sign = 1 - 2 * core
    steps = jnp.arange(RING, dtype=jnp.int32)
    at = {}
    for axis, shape in zip(order, ((1, 1, RING), (1, RING, 1), (RING, 1, 1))):
        at[axis] = jnp.mod(place[axis] - sign * steps + RING, RING).reshape(shape)
    table = (at["x"] % 2) * 32 + (at["x"] // 2) * 16 + at["z"] * 4 + at["y"]
    return jnp.broadcast_to(table, (RING, RING, RING)).reshape(RING**3)


def pack_kernel(wq, wk, wv, wo, wu, wd, *outs):
    for layer in range(2):
        attn, up, down = outs[layer * 3 : layer * 3 + 3]
        attn[:, 0:256] = wq[layer]
        attn[:, 256:512] = wk[layer]
        attn[:, 512:768] = wv[layer]
        attn[:, 768:1024] = wo[layer].T
        up[...] = wu[layer]
        down[...] = wd[layer].T


def normalize(values, gain):
    mean = jnp.mean(values, axis=-1, keepdims=True)
    centered = values - mean
    spread_of = jnp.mean(centered * centered, axis=-1, keepdims=True)
    return centered * lax.rsqrt(spread_of + EPSILON) * gain


def settle(base, own, other, gain):
    total = own[...].astype(jnp.float32) + other[...].astype(jnp.float32)
    return normalize(base[...].astype(jnp.float32) + total, gain[...]).astype(jnp.bfloat16)


def fetch(table, blocks, store, sems):
    for third in range(RING):
        def one(index, carry, third=third):
            to = table[third * 16 + index]
            half = to // 32
            pltpu.make_async_copy(
                blocks[third].at[index], store.at[half, to % 32], sems.at[half]
            ).start()
            return carry

        lax.fori_loop(0, 16, one, 0)


def arrived(store, half, sems):
    pltpu.make_async_copy(store.at[half], store.at[half], sems.at[half]).wait()


def attention_kernel(fresh, table, seg_col, seg_row, base, own, other, gain, b0, b1, b2, b3, *rest):
    if fresh:
        term, store, bias, sems = rest
    else:
        hidden_out, term, store, bias, sems = rest
    fetch(table, (b0, b1, b2, b3), store, sems)
    bias[...] = jnp.where(seg_col[...] == seg_row[...], 0.0, -1e30)
    if fresh:
        hidden = base[...]
    else:
        hidden = settle(base, own, other, gain)
        hidden_out[...] = hidden
    lane = lax.broadcasted_iota(jnp.int32, (1, 128), 1)
    ones = jnp.ones((BIN, 128), jnp.bfloat16)
    total = None
    for half in range(2):
        arrived(store, half, sems)
        weights = store[half].reshape(D, D)
        qkv = jnp.dot(hidden, weights[:, :768], preferred_element_type=jnp.float32)
        qkv = qkv.astype(jnp.bfloat16)
        contexts = []
        for pair in range(2):
            query = qkv[:, pair * 128 : pair * 128 + 128]
            keys = qkv[:, 256 + pair * 128 : 256 + pair * 128 + 128]
            values = qkv[:, 512 + pair * 128 : 512 + pair * 128 + 128]
            values = jnp.concatenate([values, ones], axis=1)
            rows = []
            for part in range(2):
                span = slice(part * 256, part * 256 + 256)
                both = []
                for head in range(2):
                    mine = (lane < HEAD) if head == 0 else (lane >= HEAD)
                    one = jnp.where(mine, query[span], jnp.zeros((), jnp.bfloat16))
                    scores = lax.dot_general(one, keys, NT, preferred_element_type=jnp.float32)
                    scores = scores + bias[span, :]
                    highest = jnp.max(scores, axis=-1, keepdims=True)
                    probs = jnp.exp2((scores - highest) * (LOG2E * HEAD**-0.5))
                    mixed = jnp.dot(
                        probs.astype(jnp.bfloat16), values, preferred_element_type=jnp.float32
                    )
                    both.append(mixed[:, :128] / mixed[:, 128:])
                rows.append(jnp.where(lane < HEAD, both[0], both[1]).astype(jnp.bfloat16))
            contexts.append(jnp.concatenate(rows, axis=0))
        context = jnp.concatenate(contexts, axis=1)
        piece = lax.dot_general(context, weights[:, 768:], NT, preferred_element_type=jnp.float32)
        total = piece if total is None else total + piece
    term[...] = total.astype(jnp.bfloat16)


def gelu(values):
    return 0.5 * values * (1.0 + lax.erf(values * (0.5**0.5)))


def ffn_kernel(table_up, table_down, base, own, other, gain, u0, u1, u2, u3, d0, d1, d2, d3,
               mixed_out, term, up_store, down_store, total, up_sems, down_sems):
    fetch(table_up, (u0, u1, u2, u3), up_store, up_sems)
    fetch(table_down, (d0, d1, d2, d3), down_store, down_sems)
    mixed = settle(base, own, other, gain)
    mixed_out[...] = mixed
    width = 512
    for half in range(2):
        arrived(up_store, half, up_sems)
        arrived(down_store, half, down_sems)
        up = up_store[half].reshape(D, D)
        down = down_store[half].reshape(D, D)
        for cut in range(D // width):
            span = slice(cut * width, cut * width + width)
            raised = jnp.dot(mixed, up[:, span], preferred_element_type=jnp.float32)
            active = gelu(raised).astype(jnp.bfloat16)
            piece = lax.dot_general(active, down[:, span], NT, preferred_element_type=jnp.float32)
            if half == 0 and cut == 0:
                total[...] = piece
            else:
                total[...] += piece
    term[...] = total[...].astype(jnp.bfloat16)


def pool_kernel(pieces_of, member, counts, placing, base, own, other, gain, *rest):
    outs, store = rest[:RING], rest[RING]
    hidden = settle(base, own, other, gain)
    sums = jnp.dot(member[...], hidden, preferred_element_type=jnp.float32)
    pooled = (sums / counts[...]).astype(jnp.bfloat16)
    for piece in range(4):
        store[piece] = pooled[:, piece * 256 : piece * 256 + 256]
    for step in range(RING):
        mine = store[pieces_of[step]]
        for rank in range(2):
            rows = jnp.dot(placing[step, rank], mine, preferred_element_type=jnp.float32)
            outs[step][:, rank * 256 : rank * 256 + 256] = rows.astype(jnp.bfloat16)


def shape(dims, kind=jnp.bfloat16):
    return jax.ShapeDtypeStruct(dims, kind)


VMEM = pl.BlockSpec(memory_space=pltpu.VMEM)
SMEM = pl.BlockSpec(memory_space=pltpu.SMEM)
ANY = pl.BlockSpec(memory_space=pl.ANY)


def params(mib):
    return pltpu.CompilerParams(vmem_limit_bytes=mib * 2**20)


def passage_tables(lengths):
    ends = jnp.cumsum(lengths, axis=1)
    starts = ends - lengths
    place = jnp.arange(BIN, dtype=jnp.int32)
    segment = jnp.sum((place[None, :, None] >= ends[:, None, :]).astype(jnp.int32), axis=2)
    opening = jnp.any(
        (place[None, :, None] == starts[:, None, :]) & (lengths[:, None, :] > 0), axis=2
    )
    return segment, opening


ORDERS = {"attn": ("y", "z", "x"), "up": ("z", "x", "y"), "down": ("x", "y", "z")}


def local(hidden_in, token_ids, lengths, owners, w_query, w_key, w_value, w_out, w_up, w_down, gains):
    x_lo, x_hi, core = lax.axis_index("x_lo"), lax.axis_index("x_hi"), lax.axis_index("core")
    place = {"x": x_hi * 2 + x_lo, "y": lax.axis_index("y"), "z": lax.axis_index("z")}
    tables = {name: block_table(order, place, core) for name, order in ORDERS.items()}

    packed = pl.pallas_call(
        pack_kernel,
        out_shape=[shape((32, 1024))] * 6,
        in_specs=[VMEM] * 6,
        out_specs=[VMEM] * 6,
        name="pack",
    )(w_query, w_key, w_value, w_out, w_up, w_down)
    blocks = []
    for layer in range(2):
        blocks.append({
            name: spread(packed[layer * 3 + k], ORDERS[name])
            for k, name in enumerate(("attn", "up", "down"))
        })

    segments, openings = passage_tables(lengths)
    segment = lax.dynamic_slice_in_dim(segments, x_lo, 1, 0)
    opening = lax.dynamic_slice_in_dim(openings, x_lo, 1, 0)
    ids = lax.dynamic_slice_in_dim(token_ids.reshape(2, BIN), x_lo, 1, 0)
    seg_col = segment.reshape(BIN, 1)
    keep = (ids >= SKIP_IDS) | opening
    member = (segment == jnp.arange(8, dtype=jnp.int32)[:, None]) & keep
    counts = jnp.sum(member.astype(jnp.float32), axis=1, keepdims=True)
    counts = jnp.where(counts > 0, counts, 1.0)
    member = member.astype(jnp.bfloat16)
    live = lengths.reshape(16) > 0
    owner = owners.reshape(16)
    order = jnp.arange(16, dtype=jnp.int32)
    earlier = (owner[None, :] == owner[:, None]) & live[None, :] & (order[None, :] < order[:, None])
    rank = jnp.sum(earlier.astype(jnp.int32), axis=1)
    target = jnp.where(live, rank * 32 + owner, -1)
    target = lax.dynamic_slice_in_dim(target, x_lo * 8, 8, 0)
    to_x = jnp.mod(place["x"] + jnp.arange(RING, dtype=jnp.int32), RING)
    pieces_of = (to_x % 2) * 2 + core
    rows = (
        jnp.arange(2, dtype=jnp.int32)[None, :, None] * 32
        + (to_x // 2)[:, None, None] * 16
        + jnp.arange(16, dtype=jnp.int32)[None, None, :]
    )
    placing = (rows[:, :, :, None] == target[None, None, None, :]).astype(jnp.bfloat16)

    hidden = lax.dynamic_slice_in_dim(hidden_in, x_lo * BIN, BIN, 0)
    base = own = other = hidden
    row = shape((BIN, D))
    for layer in range(2):
        fresh = layer == 0
        gain = gains[layer - 1, 1][None] if layer else gains[0, 0][None]
        result = pl.pallas_call(
            functools.partial(attention_kernel, fresh),
            out_shape=[row] if fresh else [row, row],
            in_specs=[SMEM] + [VMEM] * 6 + [ANY] * 4,
            out_specs=[VMEM] if fresh else [VMEM, VMEM],
            scratch_shapes=[
                pltpu.VMEM((2, 32, 32, 1024), jnp.bfloat16),
                pltpu.VMEM((BIN, BIN), jnp.float32),
                pltpu.SemaphoreType.DMA((2,)),
            ],
            compiler_params=params(44),
            cost_estimate=pl.CostEstimate(
                flops=3 * 10**9, bytes_accessed=8 * 2**20, transcendentals=2 * 2**20
            ),
            name="attention",
        )(tables["attn"], seg_col, segment, base, own, other, gain, *blocks[layer]["attn"])
        if not fresh:
            hidden = result[0]
        own = result[-1]
        other = swap(own)
        mixed, own = pl.pallas_call(
            ffn_kernel,
            out_shape=[row, row],
            in_specs=[SMEM] * 2 + [VMEM] * 4 + [ANY] * 8,
            out_specs=[VMEM, VMEM],
            scratch_shapes=[
                pltpu.VMEM((2, 32, 32, 1024), jnp.bfloat16),
                pltpu.VMEM((2, 32, 32, 1024), jnp.bfloat16),
                pltpu.VMEM((BIN, D), jnp.float32),
                pltpu.SemaphoreType.DMA((2,)),
                pltpu.SemaphoreType.DMA((2,)),
            ],
            compiler_params=params(44),
            cost_estimate=pl.CostEstimate(
                flops=5 * 10**9, bytes_accessed=12 * 2**20, transcendentals=2**20
            ),
            name="ffn",
        )(tables["up"], tables["down"], hidden, own, other, gains[layer, 0][None],
          *blocks[layer]["up"], *blocks[layer]["down"])
        other = swap(own)
        base = mixed

    sent = pl.pallas_call(
        pool_kernel,
        out_shape=[shape((16, 512))] * RING,
        in_specs=[SMEM] + [VMEM] * 7,
        out_specs=[VMEM] * RING,
        scratch_shapes=[pltpu.VMEM((4, 8, 256), jnp.bfloat16)],
        name="pool",
    )(pieces_of, member, counts, placing, base, own, other, gains[1, 1][None])

    got = jnp.stack([sent[0]] + [shift(sent[by], "x", by) for by in range(1, RING)])
    got = jnp.stack([got[jnp.mod(place["x"] - at, RING)] for at in range(RING)])
    rows = (got[0::2] + got[1::2]).reshape(2, 4, 4, 512)
    for axis, dim in (("y", 2), ("z", 1)):
        here = place[axis]
        parts = []
        for by in range(RING):
            piece = lax.dynamic_index_in_dim(rows, jnp.mod(here + by, RING), dim, keepdims=False)
            parts.append(shift(piece, axis, by) if by else piece)
        parts = jnp.stack(parts)
        rows = jnp.stack([parts[jnp.mod(here - at, RING)] for at in range(RING)], axis=dim)
    return rows.reshape(1, 32, 2, 256)


def solution(mesh):
    fine = Mesh(mesh.devices.reshape(2, 2, 2, 4, 4), ("x_lo", "core", "x_hi", "z", "y"))
    encode = ("x_hi", "z", "y")
    trainer = ("x_lo", "core")
    in_specs = (
        P(encode, None),
        P(encode),
        P(encode, None),
        P(encode, None),
        P(None, encode, trainer),
        P(None, encode, trainer),
        P(None, encode, trainer),
        P(None, trainer, encode),
        P(None, encode, trainer),
        P(None, trainer, encode),
        P(),
    )
    out_specs = P(encode, None, None, trainer)
    return jax.shard_map(local, mesh=fine, in_specs=in_specs, out_specs=out_specs, check_vma=False)
```

```python
import functools

import jax
import jax.numpy as jnp
from jax import lax
from jax.experimental import pallas as pl
from jax.experimental.pallas import tpu as pltpu
from jax.sharding import Mesh, PartitionSpec as P

SKIP_IDS = 2000
EPSILON = 1e-05
LOG2E = 1.4426950408889634
HEAD = 64
BIN = 512
D = 1024
RING = 4
NT = (((1,), (1,)), ((), ()))


def x_line(x, core):
    return ((x % 2) * 2 + core) * 2 + x // 2


def hop(value, axis, way=1):
    pairs = []
    for core in range(2):
        step = way if core == 0 else -way
        for at in range(RING):
            to = (at + step) % RING
            if axis == "x":
                pairs.append((x_line(at, core), x_line(to, core)))
            else:
                pairs.append((core * RING + at, core * RING + to))
    names = ("x_lo", "core", "x_hi") if axis == "x" else ("core", axis)
    return lax.ppermute(value, names, pairs)


def swap(value):
    return lax.ppermute(value, "core", [(0, 1), (1, 0)])


def ring(value, axis):
    blocks = [value]
    for _ in range(RING - 1):
        blocks.append(hop(blocks[-1], axis))
    return blocks


def join_kernel(split, *refs):
    sems = refs[-1]
    outs = refs[3 * RING : -1]
    for part in range(3):
        for step in range(RING):
            source = refs[part * RING + step]
            if split:
                for layer in range(2):
                    target = outs[layer * 3 + part]
                    pltpu.make_async_copy(source.at[layer], target.at[step], sems).start()
            else:
                outs[part][:, step] = source[...]
    if split:
        for target in outs:
            pltpu.make_async_copy(target, target, sems).wait()


def join(rings, split):
    flat = [in_vmem(block) for blocks in rings for block in blocks]
    if split:
        out = [pltpu.HBM((RING, RING, 32, D), jnp.bfloat16)] * 6
    else:
        out = [pltpu.VMEM((2, RING, 32, D), jnp.bfloat16)] * 3
    return pl.pallas_call(
        functools.partial(join_kernel, split),
        out_shape=out,
        in_specs=[VMEM] * 12,
        out_specs=[HBM if split else VMEM] * len(out),
        scratch_shapes=[pltpu.SemaphoreType.DMA(())],
        compiler_params=params(16),
        cost_estimate=pl.CostEstimate(flops=0, bytes_accessed=2 * 2**20, transcendentals=0),
        name="join",
    )(*flat)


def rings(values, axes, short=False):
    one = [hop(value, axis) for value, axis in zip(values, axes)]
    two = [hop(value, axis) for value, axis in zip(one, axes)]
    if short:
        three = [hop(value, axis, -1) for value, axis in zip(values, axes)]
    else:
        three = [hop(value, axis) for value, axis in zip(two, axes)]
    return [list(blocks) for blocks in zip(values, one, two, three)]


def spread(parts, orders):
    axes = [[order[k] for order in orders] for k in range(3)]
    second = rings(join(rings(parts, axes[0], True), False), axes[1], True)
    whole = [value.reshape(RING * RING, 32, D) for value in join(second, True)]
    return [rings(whole[3 * layer : 3 * layer + 3], axes[2]) for layer in range(2)]


def block_table(order, place, core):
    sign = 1 - 2 * core
    steps = jnp.arange(RING, dtype=jnp.int32)
    at = {}
    for axis, way, dims in zip(order, (sign, sign, sign), ((1, 1, RING), (1, RING, 1), (RING, 1, 1))):
        at[axis] = jnp.mod(place[axis] - way * steps + RING, RING).reshape(dims)
    table = (at["x"] // 2) * 16 + at["z"] * 4 + at["y"]
    return jnp.broadcast_to(table, (RING, RING, RING)).reshape(RING**3)


def pack_kernel(wq, wk, wv, wo, wu, wd, attn, up, down):
    for layer in range(2):
        attn[layer, :, 0:256] = wq[layer]
        attn[layer, :, 256:512] = wk[layer]
        attn[layer, :, 512:768] = wv[layer]
        attn[layer, :, 768:1024] = wo[layer]
        up[layer] = wu[layer]
        down[layer] = wd[layer]


def normalize(values, gain):
    mean = jnp.mean(values, axis=-1, keepdims=True)
    centered = values - mean
    spread_of = jnp.mean(centered * centered, axis=-1, keepdims=True)
    return centered * lax.rsqrt(spread_of + EPSILON) * gain


def settle(base, own, other, gain):
    total = own[...].astype(jnp.float32) + other[...].astype(jnp.float32)
    return normalize(base[...].astype(jnp.float32) + total, gain[...]).astype(jnp.bfloat16)


def fetch(order, half, table, blocks, store, sems):
    spans = [range(RING)] * 3
    spans[order.index("x")] = range(half, RING, 2)
    for third in spans[2]:
        for second in spans[1]:
            for first in spans[0]:
                index = second * RING + first
                to = table[third * RING * RING + index]
                pltpu.make_async_copy(
                    blocks[third].at[index], store.at[half, to], sems.at[half]
                ).start()


def arrived(store, half, sems):
    pltpu.make_async_copy(store.at[half], store.at[half], sems.at[half]).wait()


def attention_kernel(layer, table, seg_col, seg_row, base, own, other, gain, *rest):
    fresh = layer == 0
    blocks, rest = rest[:4], rest[4:]
    if fresh:
        term, store, bias, sems = rest
    else:
        hidden_out, term, store, bias, sems = rest
    for half in range(2):
        fetch(ORDERS["attn"], half, table, blocks, store, sems)
    bias[...] = jnp.where(seg_col[...] == seg_row[...], 0.0, -1e30)
    if fresh:
        hidden = base[...]
    else:
        hidden = settle(base, own, other, gain)
        hidden_out[...] = hidden
    lane = lax.broadcasted_iota(jnp.int32, (1, 128), 1)
    ones = jnp.ones((BIN, 128), jnp.bfloat16)
    total = None
    for half in range(2):
        arrived(store, half, sems)
        weights = store[half].reshape(D, D)
        qkv = jnp.dot(hidden, weights[:, :768], preferred_element_type=jnp.float32)
        qkv = qkv.astype(jnp.bfloat16)
        contexts = []
        for pair in range(2):
            query = qkv[:, pair * 128 : pair * 128 + 128]
            keys = qkv[:, 256 + pair * 128 : 256 + pair * 128 + 128]
            values = qkv[:, 512 + pair * 128 : 512 + pair * 128 + 128]
            values = jnp.concatenate([values, ones], axis=1)
            rows = []
            for part in range(2):
                span = slice(part * 256, part * 256 + 256)
                both = []
                for head in range(2):
                    mine = (lane < HEAD) if head == 0 else (lane >= HEAD)
                    one = jnp.where(mine, query[span], jnp.zeros((), jnp.bfloat16))
                    scores = lax.dot_general(one, keys, NT, preferred_element_type=jnp.float32)
                    scores = scores + bias[span, :]
                    highest = jnp.max(scores, axis=-1, keepdims=True)
                    probs = jnp.exp2((scores - highest) * (LOG2E * HEAD**-0.5))
                    mixed = jnp.dot(
                        probs.astype(jnp.bfloat16), values, preferred_element_type=jnp.float32
                    )
                    both.append(mixed[:, :128] / mixed[:, 128:])
                rows.append(jnp.where(lane < HEAD, both[0], both[1]).astype(jnp.bfloat16))
            contexts.append(jnp.concatenate(rows, axis=0))
        context = jnp.concatenate(contexts, axis=1)
        piece = lax.dot_general(context, weights[:, 768:], NT, preferred_element_type=jnp.float32)
        total = piece if total is None else total + piece
    term[...] = total.astype(jnp.bfloat16)


def gelu(values):
    return 0.5 * values * (1.0 + lax.erf(values * (0.5**0.5)))


def ffn_kernel(layer, table_up, table_down, base, own, other, gain, *rest):
    up_blocks, down_blocks, rest = rest[:4], rest[4:8], rest[8:]
    mixed_out, term, up_store, down_store, total, active, up_sems, down_sems = rest
    for half in range(2):
        fetch(ORDERS["up"], half, table_up, up_blocks, up_store, up_sems)
        fetch(ORDERS["down"], half, table_down, down_blocks, down_store, down_sems)
    mixed = settle(base, own, other, gain)
    mixed_out[...] = mixed
    width = 512
    for half in range(2):
        arrived(up_store, half, up_sems)
        up = up_store[half].reshape(D, D)
        for cut in range(D // width):
            span = slice(cut * width, cut * width + width)
            raised = jnp.dot(mixed, up[:, span], preferred_element_type=jnp.float32)
            active[:, span] = gelu(raised).astype(jnp.bfloat16)
        arrived(down_store, half, down_sems)
        down = down_store[half].reshape(D, D)
        for cut in range(D // width):
            span = slice(cut * width, cut * width + width)
            piece = lax.dot_general(active[...], down[span, :], NT, preferred_element_type=jnp.float32)
            if half == 0:
                total[:, span] = piece
            else:
                term[:, span] = (total[:, span] + piece).astype(jnp.bfloat16)


def pool_kernel(core, member, counts, placing, base, own, other, gain, out, store):
    hidden = settle(base, own, other, gain)
    sums = jnp.dot(member[...], hidden, preferred_element_type=jnp.float32)
    pooled = (sums / counts[...]).astype(jnp.bfloat16)
    for piece in range(4):
        store[piece] = pooled[:, piece * 256 : piece * 256 + 256]
    for column in range(2):
        mine = store[column * 2 + core[0]]
        for rank in range(2):
            rows = jnp.dot(placing[rank], mine, preferred_element_type=jnp.float32)
            out[column, :, rank, :] = rows.astype(jnp.bfloat16)


def shape(dims, kind=jnp.bfloat16):
    return jax.ShapeDtypeStruct(dims, kind)


VMEM = pl.BlockSpec(memory_space=pltpu.VMEM)
SMEM = pl.BlockSpec(memory_space=pltpu.SMEM)
HBM = pl.BlockSpec(memory_space=pltpu.HBM)


def in_hbm(blocks):
    return [pltpu.with_memory_space_constraint(block, pltpu.HBM) for block in blocks]


def in_vmem(value):
    return pltpu.with_memory_space_constraint(value, pltpu.VMEM)


def params(mib):
    return pltpu.CompilerParams(vmem_limit_bytes=mib * 2**20)


def passage_tables(lengths):
    ends = jnp.cumsum(lengths, axis=1)
    starts = ends - lengths
    place = jnp.arange(BIN, dtype=jnp.int32)
    segment = jnp.sum((place[None, :, None] >= ends[:, None, :]).astype(jnp.int32), axis=2)
    opening = jnp.any(
        (place[None, :, None] == starts[:, None, :]) & (lengths[:, None, :] > 0), axis=2
    )
    return segment, opening


ORDERS = {"attn": ("y", "z", "x"), "up": ("z", "x", "y"), "down": ("x", "y", "z")}


def local(hidden_in, token_ids, lengths, owners, w_query, w_key, w_value, w_out, w_up, w_down, gains):
    x_lo, x_hi, core = lax.axis_index("x_lo"), lax.axis_index("x_hi"), lax.axis_index("core")
    place = {"x": x_hi * 2 + x_lo, "y": lax.axis_index("y"), "z": lax.axis_index("z")}
    tables = {name: block_table(order, place, core) for name, order in ORDERS.items()}

    packed = pl.pallas_call(
        pack_kernel,
        out_shape=[pltpu.VMEM((2, 32, D), jnp.bfloat16)] * 3,
        in_specs=[VMEM] * 6,
        out_specs=[VMEM] * 3,
        name="pack",
    )(w_query, w_key, w_value, jnp.swapaxes(w_out, 1, 2), w_up, jnp.swapaxes(w_down, 1, 2))
    names = ("attn", "up", "down")
    blocks = [dict(zip(names, of)) for of in spread(packed, [ORDERS[name] for name in names])]

    segments, openings = passage_tables(lengths)
    segment = lax.dynamic_slice_in_dim(segments, x_lo, 1, 0)
    opening = lax.dynamic_slice_in_dim(openings, x_lo, 1, 0)
    ids = lax.dynamic_slice_in_dim(token_ids.reshape(2, BIN), x_lo, 1, 0)
    seg_col = segment.reshape(BIN, 1)
    keep = (ids >= SKIP_IDS) | opening
    member = (segment == jnp.arange(8, dtype=jnp.int32)[:, None]) & keep
    counts = jnp.sum(member.astype(jnp.float32), axis=1, keepdims=True)
    counts = jnp.where(counts > 0, counts, 1.0)
    member = member.astype(jnp.bfloat16)
    live = lengths.reshape(16) > 0
    owner = owners.reshape(16)
    order = jnp.arange(16, dtype=jnp.int32)
    earlier = (owner[None, :] == owner[:, None]) & live[None, :] & (order[None, :] < order[:, None])
    rank = jnp.sum(earlier.astype(jnp.int32), axis=1)
    target = jnp.where(live, rank * 32 + owner, -1)
    target = lax.dynamic_slice_in_dim(target, x_lo * 8, 8, 0)
    rows = jnp.arange(64, dtype=jnp.int32)
    placing = (rows[:, None] == target[None, :]).astype(jnp.bfloat16).reshape(2, 32, 8)

    hidden = lax.dynamic_slice_in_dim(hidden_in, x_lo * BIN, BIN, 0)
    hidden, tables, gains, seg_col, segment, member, counts, placing, core = lax.optimization_barrier(
        (hidden, tables, gains, seg_col, segment, member, counts, placing, core.reshape(1))
    )
    base = own = other = hidden
    row = pltpu.VMEM((BIN, D), jnp.bfloat16)
    for layer in range(2):
        fresh = layer == 0
        gain = gains[layer - 1, 1][None] if layer else gains[0, 0][None]
        result = pl.pallas_call(
            functools.partial(attention_kernel, layer),
            out_shape=[row] if fresh else [row, row],
            in_specs=[SMEM] + [VMEM] * 6 + [HBM] * 4,
            out_specs=[VMEM] if fresh else [VMEM, VMEM],
            scratch_shapes=[
                pltpu.VMEM((2, 32, 32, 1024), jnp.bfloat16),
                pltpu.VMEM((BIN, BIN), jnp.float32),
                pltpu.SemaphoreType.DMA((2,)),
            ],
            compiler_params=params(16),
            cost_estimate=pl.CostEstimate(
                flops=3 * 10**9, bytes_accessed=8 * 2**20, transcendentals=2 * 2**20
            ),
            name="attention",
        )(tables["attn"], seg_col, segment, in_vmem(base), in_vmem(own), in_vmem(other), gain, *in_hbm(blocks[layer]["attn"]))
        if not fresh:
            hidden = result[0]
        own = result[-1]
        other = swap(own)
        mixed, own = pl.pallas_call(
            functools.partial(ffn_kernel, layer),
            out_shape=[row, row],
            in_specs=[SMEM] * 2 + [VMEM] * 4 + [HBM] * 8,
            out_specs=[VMEM, VMEM],
            scratch_shapes=[
                pltpu.VMEM((2, 32, 32, 1024), jnp.bfloat16),
                pltpu.VMEM((2, 32, 32, 1024), jnp.bfloat16),
                pltpu.VMEM((BIN, D), jnp.float32),
                pltpu.VMEM((BIN, D), jnp.bfloat16),
                pltpu.SemaphoreType.DMA((2,)),
                pltpu.SemaphoreType.DMA((2,)),
            ],
            compiler_params=params(16),
            cost_estimate=pl.CostEstimate(
                flops=5 * 10**9, bytes_accessed=12 * 2**20, transcendentals=2**20
            ),
            name="ffn",
        )(tables["up"], tables["down"], in_vmem(hidden), in_vmem(own), in_vmem(other), gains[layer, 0][None],
          *in_hbm(blocks[layer]["up"]), *in_hbm(blocks[layer]["down"]))
        other = swap(own)
        base = mixed

    sent = pl.pallas_call(
        pool_kernel,
        out_shape=shape((2, 32, 2, 256)),
        in_specs=[SMEM] + [VMEM] * 7,
        out_specs=VMEM,
        scratch_shapes=[pltpu.VMEM((4, 8, 256), jnp.bfloat16)],
        compiler_params=params(16),
        name="pool",
    )(core, member, counts, placing, in_vmem(base), in_vmem(own), in_vmem(other), gains[1, 1][None])

    names = ("x_lo", "x_hi", "z", "y")
    got = lax.all_to_all(sent.reshape(64, 2, 256), names, split_axis=0, concat_axis=0, tiled=True)
    got = got.reshape(2, 1, 32, 2, 256)
    return got[0] + got[1]


def solution(mesh):
    fine = Mesh(mesh.devices.reshape(2, 2, 2, 4, 4), ("x_lo", "core", "x_hi", "z", "y"))
    encode = ("x_hi", "z", "y")
    trainer = ("x_lo", "core")
    in_specs = (
        P(encode, None),
        P(encode),
        P(encode, None),
        P(encode, None),
        P(None, encode, trainer),
        P(None, encode, trainer),
        P(None, encode, trainer),
        P(None, trainer, encode),
        P(None, encode, trainer),
        P(None, trainer, encode),
        P(),
    )
    out_specs = P(encode, None, None, trainer)
    return jax.shard_map(local, mesh=fine, in_specs=in_specs, out_specs=out_specs, check_vma=False)
```

```python
import functools

import jax
import jax.numpy as jnp
from jax import lax
from jax.experimental import pallas as pl
from jax.experimental.pallas import tpu as pltpu
from jax.sharding import Mesh, PartitionSpec as P

SKIP_IDS = 2000
EPSILON = 1e-05
LOG2E = 1.4426950408889634
HEAD = 64
BIN = 512
D = 1024
RING = 4
NT = (((1,), (1,)), ((), ()))


def x_line(x, core):
    return ((x % 2) * 2 + core) * 2 + x // 2


def hop(value, axis, way=1):
    pairs = []
    for core in range(2):
        step = way if core == 0 else -way
        for at in range(RING):
            to = (at + step) % RING
            if axis == "x":
                pairs.append((x_line(at, core), x_line(to, core)))
            else:
                pairs.append((core * RING + at, core * RING + to))
    names = ("x_lo", "core", "x_hi") if axis == "x" else ("core", axis)
    return lax.ppermute(value, names, pairs)


def swap(value):
    return lax.ppermute(value, "core", [(0, 1), (1, 0)])


def ring(value, axis):
    blocks = [value]
    for _ in range(RING - 1):
        blocks.append(hop(blocks[-1], axis))
    return blocks


def join_kernel(split, *refs):
    outs = refs[3 * RING : -1]
    copies = []
    for part in range(3):
        for step in range(RING):
            source = refs[part * RING + step]
            if split:
                for layer in range(2):
                    target, sem = outs[layer * 3 + part].at[step], refs[-1].at[layer, part, step]
                    copies.append(pltpu.make_async_copy(source.at[layer], target, sem))
                    copies[-1].start()
            else:
                outs[part][:, step] = source[...]
    for copy in copies:
        copy.wait()


def join(rings, split):
    flat = [in_vmem(block) for blocks in rings for block in blocks]
    if split:
        out = [pltpu.HBM((RING, RING, 32, D), jnp.bfloat16)] * 6
    else:
        out = [pltpu.VMEM((2, RING, 32, D), jnp.bfloat16)] * 3
    return pl.pallas_call(
        functools.partial(join_kernel, split),
        out_shape=out,
        in_specs=[VMEM] * 12,
        out_specs=[HBM if split else VMEM] * len(out),
        scratch_shapes=[pltpu.SemaphoreType.DMA((2, 3, RING))],
        compiler_params=params(16),
        cost_estimate=pl.CostEstimate(flops=0, bytes_accessed=2 * 2**20, transcendentals=0),
        name="join",
    )(*flat)


def rings(values, axes, short=False):
    one = [hop(value, axis) for value, axis in zip(values, axes)]
    two = [hop(value, axis) for value, axis in zip(one, axes)]
    if short:
        three = [hop(value, axis, -1) for value, axis in zip(values, axes)]
    else:
        three = [hop(value, axis) for value, axis in zip(two, axes)]
    return [list(blocks) for blocks in zip(values, one, two, three)]


def spread(parts, orders):
    axes = [[order[k] for order in orders] for k in range(3)]
    second = rings(join(rings(parts, axes[0], True), False), axes[1], True)
    whole = [value.reshape(RING * RING, 32, D) for value in join(second, True)]
    return [rings(whole[3 * layer : 3 * layer + 3], axes[2]) for layer in range(2)]


def block_table(order, place, core):
    sign = 1 - 2 * core
    steps = jnp.arange(RING, dtype=jnp.int32)
    at = {}
    for axis, way, dims in zip(order, (sign, sign, sign), ((1, 1, RING), (1, RING, 1), (RING, 1, 1))):
        at[axis] = jnp.mod(place[axis] - way * steps + RING, RING).reshape(dims)
    table = (at["x"] // 2) * 16 + at["z"] * 4 + at["y"]
    return jnp.broadcast_to(table, (RING, RING, RING)).reshape(RING**3)


def pack_kernel(wq, wk, wv, wo, wu, wd, attn, up, down):
    for layer in range(2):
        attn[layer, :, 0:256] = wq[layer]
        attn[layer, :, 256:512] = wk[layer]
        attn[layer, :, 512:768] = wv[layer]
        attn[layer, :, 768:1024] = wo[layer]
        up[layer] = wu[layer]
        down[layer] = wd[layer]


def normalize(values, gain):
    mean = jnp.mean(values, axis=-1, keepdims=True)
    centered = values - mean
    spread_of = jnp.mean(centered * centered, axis=-1, keepdims=True)
    return centered * lax.rsqrt(spread_of + EPSILON) * gain


def settle(base, own, other, gain):
    total = own[...].astype(jnp.float32) + other[...].astype(jnp.float32)
    return normalize(base[...].astype(jnp.float32) + total, gain[...]).astype(jnp.bfloat16)


def indices(order, half):
    spans = [range(RING)] * 3
    spans[order.index("x")] = range(half, RING, 2)
    return [(t, s * RING + f) for t in spans[2] for s in spans[1] for f in spans[0]]


def fetch(order, half, table, blocks, store, sems):
    for third, index in indices(order, half):
        to = table[third * RING * RING + index]
        pltpu.make_async_copy(blocks[third].at[index], store.at[half, to], sems.at[half]).start()


def place(order, half, table, blocks, store, sems):
    if sems is None:
        for third, index in indices(order, half):
            store[half, table[third * RING * RING + index]] = blocks[third][index]
    else:
        pltpu.make_async_copy(store.at[half], store.at[half], sems.at[half]).wait()
    return store[half].reshape(D, D)


def attention_kernel(layer, table, seg_col, seg_row, base, own, other, gain, *rest):
    fresh = layer == 0
    blocks, rest = rest[:4], rest[4:]
    if fresh:
        term, store, bias, sems = rest
        for half in range(2):
            fetch(ORDERS["attn"], half, table, blocks, store, sems)
    else:
        hidden_out, term, store, bias = rest
        sems = None
    bias[...] = jnp.where(seg_col[...] == seg_row[...], 0.0, -1e30)
    if fresh:
        hidden = base[...]
    else:
        hidden = settle(base, own, other, gain)
        hidden_out[...] = hidden
    lane = lax.broadcasted_iota(jnp.int32, (1, 128), 1)
    ones = jnp.ones((BIN, 128), jnp.bfloat16)
    total = None
    for half in range(2):
        weights = place(ORDERS["attn"], half, table, blocks, store, sems)
        qkv = jnp.dot(hidden, weights[:, :768], preferred_element_type=jnp.float32)
        qkv = qkv.astype(jnp.bfloat16)
        contexts = []
        for pair in range(2):
            query = qkv[:, pair * 128 : pair * 128 + 128]
            keys = qkv[:, 256 + pair * 128 : 256 + pair * 128 + 128]
            values = qkv[:, 512 + pair * 128 : 512 + pair * 128 + 128]
            values = jnp.concatenate([values, ones], axis=1)
            rows = []
            for part in range(2):
                span = slice(part * 256, part * 256 + 256)
                both = []
                for head in range(2):
                    mine = (lane < HEAD) if head == 0 else (lane >= HEAD)
                    one = jnp.where(mine, query[span], jnp.zeros((), jnp.bfloat16))
                    scores = lax.dot_general(one, keys, NT, preferred_element_type=jnp.float32)
                    scores = scores + bias[span, :]
                    highest = jnp.max(scores, axis=-1, keepdims=True)
                    probs = jnp.exp2((scores - highest) * (LOG2E * HEAD**-0.5))
                    mixed = jnp.dot(
                        probs.astype(jnp.bfloat16), values, preferred_element_type=jnp.float32
                    )
                    both.append(mixed[:, :128] / mixed[:, 128:])
                rows.append(jnp.where(lane < HEAD, both[0], both[1]).astype(jnp.bfloat16))
            contexts.append(jnp.concatenate(rows, axis=0))
        context = jnp.concatenate(contexts, axis=1)
        piece = lax.dot_general(context, weights[:, 768:], NT, preferred_element_type=jnp.float32)
        total = piece if total is None else total + piece
    term[...] = total.astype(jnp.bfloat16)


def gelu(values):
    return 0.5 * values * (1.0 + lax.erf(values * (0.5**0.5)))


def ffn_kernel(layer, table_up, table_down, base, own, other, gain, *rest):
    up_blocks, down_blocks, rest = rest[:4], rest[4:8], rest[8:]
    mixed_out, term, up_store, down_store, total, active, *sems = rest
    up_sems, down_sems = sems or (None, None)
    if sems:
        for half in range(2):
            fetch(ORDERS["up"], half, table_up, up_blocks, up_store, up_sems)
            fetch(ORDERS["down"], half, table_down, down_blocks, down_store, down_sems)
    mixed = settle(base, own, other, gain)
    mixed_out[...] = mixed
    width = 512
    for half in range(2):
        up = place(ORDERS["up"], half, table_up, up_blocks, up_store, up_sems)
        for cut in range(D // width):
            span = slice(cut * width, cut * width + width)
            raised = jnp.dot(mixed, up[:, span], preferred_element_type=jnp.float32)
            active[:, span] = gelu(raised).astype(jnp.bfloat16)
        down = place(ORDERS["down"], half, table_down, down_blocks, down_store, down_sems)
        for cut in range(D // width):
            span = slice(cut * width, cut * width + width)
            piece = lax.dot_general(active[...], down[span, :], NT, preferred_element_type=jnp.float32)
            if half == 0:
                total[:, span] = piece
            else:
                term[:, span] = (total[:, span] + piece).astype(jnp.bfloat16)


def pool_kernel(core, member, counts, placing, base, own, other, gain, out, store):
    hidden = settle(base, own, other, gain)
    sums = jnp.dot(member[...], hidden, preferred_element_type=jnp.float32)
    pooled = (sums / counts[...]).astype(jnp.bfloat16)
    for piece in range(4):
        store[piece] = pooled[:, piece * 256 : piece * 256 + 256]
    for column in range(2):
        mine = store[column * 2 + core[0]]
        for rank in range(2):
            rows = jnp.dot(placing[rank], mine, preferred_element_type=jnp.float32)
            out[column, :, rank, :] = rows.astype(jnp.bfloat16)


def shape(dims, kind=jnp.bfloat16):
    return jax.ShapeDtypeStruct(dims, kind)


VMEM = pl.BlockSpec(memory_space=pltpu.VMEM)
HBM = pl.BlockSpec(memory_space=pltpu.HBM)
SMEM = pl.BlockSpec(memory_space=pltpu.SMEM)


def in_hbm(value):
    return pltpu.with_memory_space_constraint(value, pltpu.HBM)


def in_vmem(value):
    return pltpu.with_memory_space_constraint(value, pltpu.VMEM)


def params(mib):
    return pltpu.CompilerParams(vmem_limit_bytes=mib * 2**20)


def passage_tables(lengths):
    ends = jnp.cumsum(lengths, axis=1)
    starts = ends - lengths
    place = jnp.arange(BIN, dtype=jnp.int32)
    segment = jnp.sum((place[None, :, None] >= ends[:, None, :]).astype(jnp.int32), axis=2)
    opening = jnp.any(
        (place[None, :, None] == starts[:, None, :]) & (lengths[:, None, :] > 0), axis=2
    )
    return segment, opening


ORDERS = {"attn": ("y", "z", "x"), "up": ("z", "x", "y"), "down": ("x", "y", "z")}


def local(hidden_in, token_ids, lengths, owners, w_query, w_key, w_value, w_out, w_up, w_down, gains):
    x_lo, x_hi, core = lax.axis_index("x_lo"), lax.axis_index("x_hi"), lax.axis_index("core")
    place = {"x": x_hi * 2 + x_lo, "y": lax.axis_index("y"), "z": lax.axis_index("z")}
    tables = {name: block_table(order, place, core) for name, order in ORDERS.items()}

    packed = pl.pallas_call(
        pack_kernel,
        out_shape=[pltpu.VMEM((2, 32, D), jnp.bfloat16)] * 3,
        in_specs=[VMEM] * 6,
        out_specs=[VMEM] * 3,
        name="pack",
    )(w_query, w_key, w_value, jnp.swapaxes(w_out, 1, 2), w_up, jnp.swapaxes(w_down, 1, 2))
    names = ("attn", "up", "down")
    blocks = [dict(zip(names, of)) for of in spread(packed, [ORDERS[name] for name in names])]

    segments, openings = passage_tables(lengths)
    segment = lax.dynamic_slice_in_dim(segments, x_lo, 1, 0)
    opening = lax.dynamic_slice_in_dim(openings, x_lo, 1, 0)
    ids = lax.dynamic_slice_in_dim(token_ids.reshape(2, BIN), x_lo, 1, 0)
    seg_col = segment.reshape(BIN, 1)
    keep = (ids >= SKIP_IDS) | opening
    member = (segment == jnp.arange(8, dtype=jnp.int32)[:, None]) & keep
    counts = jnp.sum(member.astype(jnp.float32), axis=1, keepdims=True)
    counts = jnp.where(counts > 0, counts, 1.0)
    member = member.astype(jnp.bfloat16)
    live = lengths.reshape(16) > 0
    owner = owners.reshape(16)
    order = jnp.arange(16, dtype=jnp.int32)
    earlier = (owner[None, :] == owner[:, None]) & live[None, :] & (order[None, :] < order[:, None])
    rank = jnp.sum(earlier.astype(jnp.int32), axis=1)
    target = jnp.where(live, rank * 32 + owner, -1)
    target = lax.dynamic_slice_in_dim(target, x_lo * 8, 8, 0)
    rows = jnp.arange(64, dtype=jnp.int32)
    placing = (rows[:, None] == target[None, :]).astype(jnp.bfloat16).reshape(2, 32, 8)

    hidden = lax.dynamic_slice_in_dim(hidden_in, x_lo * BIN, BIN, 0)
    hidden, tables, gains, seg_col, segment, member, counts, placing, core = lax.optimization_barrier(
        (hidden, tables, gains, seg_col, segment, member, counts, placing, core.reshape(1))
    )
    base = own = other = hidden
    row = pltpu.VMEM((BIN, D), jnp.bfloat16)
    for layer in range(2):
        fresh = layer == 0
        spec, hold = (HBM, in_hbm) if fresh else (VMEM, in_vmem)
        sems = [pltpu.SemaphoreType.DMA((2,))] if fresh else []
        gain = gains[layer - 1, 1][None] if layer else gains[0, 0][None]
        result = pl.pallas_call(
            functools.partial(attention_kernel, layer),
            out_shape=[row] if fresh else [row, row],
            in_specs=[SMEM] + [VMEM] * 6 + [spec] * 4,
            out_specs=[VMEM] if fresh else [VMEM, VMEM],
            scratch_shapes=[
                pltpu.VMEM((2, 32, 32, 1024), jnp.bfloat16),
                pltpu.VMEM((BIN, BIN), jnp.float32),
            ] + sems,
            compiler_params=params(16),
            cost_estimate=pl.CostEstimate(
                flops=3 * 10**9, bytes_accessed=8 * 2**20, transcendentals=2 * 2**20
            ),
            name="attention",
        )(tables["attn"], seg_col, segment, in_vmem(base), in_vmem(own), in_vmem(other), gain, *map(hold, blocks[layer]["attn"]))
        if not fresh:
            hidden = result[0]
        own = result[-1]
        other = swap(own)
        mixed, own = pl.pallas_call(
            functools.partial(ffn_kernel, layer),
            out_shape=[row, row],
            in_specs=[SMEM] * 2 + [VMEM] * 4 + [spec] * 8,
            out_specs=[VMEM, VMEM],
            scratch_shapes=[
                pltpu.VMEM((2, 32, 32, 1024), jnp.bfloat16),
                pltpu.VMEM((2, 32, 32, 1024), jnp.bfloat16),
                pltpu.VMEM((BIN, D), jnp.float32),
                pltpu.VMEM((BIN, D), jnp.bfloat16),
            ] + sems * 2,
            compiler_params=params(16),
            cost_estimate=pl.CostEstimate(
                flops=5 * 10**9, bytes_accessed=12 * 2**20, transcendentals=2**20
            ),
            name="ffn",
        )(tables["up"], tables["down"], in_vmem(hidden), in_vmem(own), in_vmem(other), gains[layer, 0][None],
          *map(hold, blocks[layer]["up"] + blocks[layer]["down"]))
        other = swap(own)
        base = mixed

    sent = pl.pallas_call(
        pool_kernel,
        out_shape=shape((2, 32, 2, 256)),
        in_specs=[SMEM] + [VMEM] * 7,
        out_specs=VMEM,
        scratch_shapes=[pltpu.VMEM((4, 8, 256), jnp.bfloat16)],
        compiler_params=params(16),
        name="pool",
    )(core, member, counts, placing, in_vmem(base), in_vmem(own), in_vmem(other), gains[1, 1][None])

    names = ("x_lo", "x_hi", "z", "y")
    got = lax.all_to_all(sent.reshape(64, 2, 256), names, split_axis=0, concat_axis=0, tiled=True)
    got = got.reshape(2, 1, 32, 2, 256)
    return got[0] + got[1]


def solution(mesh):
    fine = Mesh(mesh.devices.reshape(2, 2, 2, 4, 4), ("x_lo", "core", "x_hi", "z", "y"))
    encode = ("x_hi", "z", "y")
    trainer = ("x_lo", "core")
    in_specs = (
        P(encode, None),
        P(encode),
        P(encode, None),
        P(encode, None),
        P(None, encode, trainer),
        P(None, encode, trainer),
        P(None, encode, trainer),
        P(None, trainer, encode),
        P(None, encode, trainer),
        P(None, trainer, encode),
        P(),
    )
    out_specs = P(encode, None, None, trainer)
    return jax.shard_map(local, mesh=fine, in_specs=in_specs, out_specs=out_specs, check_vma=False)
```

```python
import functools

import jax
import jax.numpy as jnp
from jax import lax
from jax.experimental import pallas as pl
from jax.experimental.pallas import tpu as pltpu
from jax.sharding import Mesh, PartitionSpec as P

SKIP_IDS = 2000
EPSILON = 1e-05
LOG2E = 1.4426950408889634
HEAD = 64
BIN = 512
D = 1024
RING = 4
NT = (((1,), (1,)), ((), ()))


def x_line(x, core):
    return ((x % 2) * 2 + core) * 2 + x // 2


def hop(value, axis, way=1):
    pairs = []
    for core in range(2):
        step = way if core == 0 else -way
        for at in range(RING):
            to = (at + step) % RING
            if axis == "x":
                pairs.append((x_line(at, core), x_line(to, core)))
            else:
                pairs.append((core * RING + at, core * RING + to))
    names = ("x_lo", "core", "x_hi") if axis == "x" else ("core", axis)
    return lax.ppermute(value, names, pairs)


def swap(value):
    return lax.ppermute(value, "core", [(0, 1), (1, 0)])


def ring(value, axis):
    blocks = [value]
    for _ in range(RING - 1):
        blocks.append(hop(blocks[-1], axis))
    return blocks


def join_kernel(*refs):
    for part in range(3):
        for step in range(RING):
            refs[3 * RING + part][:, step] = refs[part * RING + step][...]


def join(rings):
    flat = [in_vmem(block) for blocks in rings for block in blocks]
    return pl.pallas_call(
        join_kernel,
        out_shape=[pltpu.VMEM((2, RING, 32, D), jnp.bfloat16)] * 3,
        in_specs=[VMEM] * 12,
        out_specs=[VMEM] * 3,
        compiler_params=params(16),
        name="join",
    )(*flat)


def part_kernel(steps, *refs):
    outs = refs[-7:-1]
    copies = []
    for part in range(3):
        for k, step in enumerate(steps):
            source = refs[part * len(steps) + k]
            for layer in range(2):
                target, sem = outs[layer * 3 + part].at[step], refs[-1].at[layer, part, k]
                copies.append(pltpu.make_async_copy(source.at[layer], target, sem))
                copies[-1].start()
    for copy in copies:
        copy.wait()


def part_join(rings, steps, whole=()):
    flat = [in_vmem(blocks[step]) for blocks in rings for step in steps]
    return pl.pallas_call(
        functools.partial(part_kernel, steps),
        out_shape=[pltpu.HBM((RING, RING, 32, D), jnp.bfloat16)] * 6,
        in_specs=[VMEM] * len(flat) + [HBM] * len(whole),
        out_specs=[HBM] * 6,
        input_output_aliases={len(flat) + k: k for k in range(len(whole))},
        scratch_shapes=[pltpu.SemaphoreType.DMA((2, 3, len(steps)))],
        compiler_params=params(16),
        name="join",
    )(*flat, *[in_hbm(value) for value in whole])


def rings(values, axes, short=False):
    one = [hop(value, axis) for value, axis in zip(values, axes)]
    two = [hop(value, axis) for value, axis in zip(one, axes)]
    if short:
        three = [hop(value, axis, -1) for value, axis in zip(values, axes)]
    else:
        three = [hop(value, axis) for value, axis in zip(two, axes)]
    return [list(blocks) for blocks in zip(values, one, two, three)]


def spread(parts, orders):
    axes = [[order[k] for order in orders] for k in range(3)]
    second = rings(join(rings(parts, axes[0], True)), axes[1], True)
    whole = part_join(second, (2,), part_join(second, (0, 1, 3)))
    whole = [value.reshape(RING * RING, 32, D) for value in whole]
    later = rings(whole[3:], axes[2])
    third = []
    for k, (value, axis) in enumerate(zip(whole[:3], axes[2])):
        one = hop(value, axis)
        two = hop(one, axis)
        last = two
        if k == 2:
            last, _ = lax.optimization_barrier((two, later[1][1]))
        third.append([value, one, two, hop(last, axis)])
    return [third, later]


def block_table(order, place, core):
    sign = 1 - 2 * core
    steps = jnp.arange(RING, dtype=jnp.int32)
    at = {}
    for axis, way, dims in zip(order, (sign, sign, sign), ((1, 1, RING), (1, RING, 1), (RING, 1, 1))):
        at[axis] = jnp.mod(place[axis] - way * steps + RING, RING).reshape(dims)
    table = (at["x"] // 2) * 16 + at["z"] * 4 + at["y"]
    return jnp.broadcast_to(table, (RING, RING, RING)).reshape(RING**3)


def pack_kernel(wq, wk, wv, wo, wu, wd, attn, up, down):
    for layer in range(2):
        attn[layer, :, 0:256] = wq[layer]
        attn[layer, :, 256:512] = wk[layer]
        attn[layer, :, 512:768] = wv[layer]
        attn[layer, :, 768:1024] = wo[layer]
        up[layer] = wu[layer]
        down[layer] = wd[layer]


def normalize(values, gain):
    mean = jnp.mean(values, axis=-1, keepdims=True)
    centered = values - mean
    spread_of = jnp.mean(centered * centered, axis=-1, keepdims=True)
    return centered * lax.rsqrt(spread_of + EPSILON) * gain


def settle(base, own, other, gain):
    total = own[...].astype(jnp.float32) + other[...].astype(jnp.float32)
    return normalize(base[...].astype(jnp.float32) + total, gain[...]).astype(jnp.bfloat16)


def indices(order, half):
    spans = [range(RING)] * 3
    spans[order.index("x")] = range(half, RING, 2)
    return [(t, s * RING + f) for t in spans[2] for s in spans[1] for f in spans[0]]


def fetch(order, half, table, blocks, store, sems):
    for third, index in indices(order, half):
        to = table[third * RING * RING + index]
        pltpu.make_async_copy(blocks[third].at[index], store.at[half, to], sems.at[half]).start()


def place(order, half, table, blocks, store, sems):
    if sems is None:
        for third, index in indices(order, half):
            store[half, table[third * RING * RING + index]] = blocks[third][index]
    else:
        pltpu.make_async_copy(store.at[half], store.at[half], sems.at[half]).wait()
    return store[half].reshape(D, D)


def attention_kernel(layer, table, seg_col, seg_row, base, own, other, gain, *rest):
    fresh = layer == 0
    blocks, rest = rest[:4], rest[4:]
    if fresh:
        term, store, bias, sems = rest
        for half in range(2):
            fetch(ORDERS["attn"], half, table, blocks, store, sems)
    else:
        hidden_out, term, store, bias = rest
        sems = None
    bias[...] = jnp.where(seg_col[...] == seg_row[...], 0.0, -1e30)
    if fresh:
        hidden = base[...]
    else:
        hidden = settle(base, own, other, gain)
        hidden_out[...] = hidden
    lane = lax.broadcasted_iota(jnp.int32, (1, 128), 1)
    ones = jnp.ones((BIN, 128), jnp.bfloat16)
    total = None
    for half in range(2):
        weights = place(ORDERS["attn"], half, table, blocks, store, sems)
        qkv = jnp.dot(hidden, weights[:, :768], preferred_element_type=jnp.float32)
        qkv = qkv.astype(jnp.bfloat16)
        contexts = []
        for pair in range(2):
            query = qkv[:, pair * 128 : pair * 128 + 128]
            keys = qkv[:, 256 + pair * 128 : 256 + pair * 128 + 128]
            values = qkv[:, 512 + pair * 128 : 512 + pair * 128 + 128]
            values = jnp.concatenate([values, ones], axis=1)
            rows = []
            for part in range(2):
                span = slice(part * 256, part * 256 + 256)
                both = []
                for head in range(2):
                    mine = (lane < HEAD) if head == 0 else (lane >= HEAD)
                    one = jnp.where(mine, query[span], jnp.zeros((), jnp.bfloat16))
                    scores = lax.dot_general(one, keys, NT, preferred_element_type=jnp.float32)
                    scores = scores + bias[span, :]
                    highest = jnp.max(scores, axis=-1, keepdims=True)
                    probs = jnp.exp2((scores - highest) * (LOG2E * HEAD**-0.5))
                    mixed = jnp.dot(
                        probs.astype(jnp.bfloat16), values, preferred_element_type=jnp.float32
                    )
                    both.append(mixed[:, :128] / mixed[:, 128:])
                rows.append(jnp.where(lane < HEAD, both[0], both[1]).astype(jnp.bfloat16))
            contexts.append(jnp.concatenate(rows, axis=0))
        context = jnp.concatenate(contexts, axis=1)
        piece = lax.dot_general(context, weights[:, 768:], NT, preferred_element_type=jnp.float32)
        total = piece if total is None else total + piece
    term[...] = total.astype(jnp.bfloat16)


def gelu(values):
    return 0.5 * values * (1.0 + lax.erf(values * (0.5**0.5)))


def ffn_kernel(layer, table_up, table_down, base, own, other, gain, *rest):
    up_blocks, down_blocks, rest = rest[:4], rest[4:8], rest[8:]
    mixed_out, term, up_store, down_store, total, active, *sems = rest
    up_sems, down_sems = sems or (None, None)
    if sems:
        for half in range(2):
            fetch(ORDERS["up"], half, table_up, up_blocks, up_store, up_sems)
            fetch(ORDERS["down"], half, table_down, down_blocks, down_store, down_sems)
    mixed = settle(base, own, other, gain)
    mixed_out[...] = mixed
    width = 512
    for half in range(2):
        up = place(ORDERS["up"], half, table_up, up_blocks, up_store, up_sems)
        for cut in range(D // width):
            span = slice(cut * width, cut * width + width)
            raised = jnp.dot(mixed, up[:, span], preferred_element_type=jnp.float32)
            active[:, span] = gelu(raised).astype(jnp.bfloat16)
        down = place(ORDERS["down"], half, table_down, down_blocks, down_store, down_sems)
        for cut in range(D // width):
            span = slice(cut * width, cut * width + width)
            piece = lax.dot_general(active[...], down[span, :], NT, preferred_element_type=jnp.float32)
            if half == 0:
                total[:, span] = piece
            else:
                term[:, span] = (total[:, span] + piece).astype(jnp.bfloat16)


def pool_kernel(core, member, counts, placing, base, own, other, gain, out, store):
    hidden = settle(base, own, other, gain)
    sums = jnp.dot(member[...], hidden, preferred_element_type=jnp.float32)
    pooled = (sums / counts[...]).astype(jnp.bfloat16)
    for piece in range(4):
        store[piece] = pooled[:, piece * 256 : piece * 256 + 256]
    for column in range(2):
        mine = store[column * 2 + core[0]]
        for rank in range(2):
            rows = jnp.dot(placing[rank], mine, preferred_element_type=jnp.float32)
            out[column, :, rank, :] = rows.astype(jnp.bfloat16)


def shape(dims, kind=jnp.bfloat16):
    return jax.ShapeDtypeStruct(dims, kind)


VMEM = pl.BlockSpec(memory_space=pltpu.VMEM)
HBM = pl.BlockSpec(memory_space=pltpu.HBM)
SMEM = pl.BlockSpec(memory_space=pltpu.SMEM)


def in_hbm(value):
    return pltpu.with_memory_space_constraint(value, pltpu.HBM)


def in_vmem(value):
    return pltpu.with_memory_space_constraint(value, pltpu.VMEM)


def params(mib):
    return pltpu.CompilerParams(vmem_limit_bytes=mib * 2**20)


def passage_tables(lengths):
    ends = jnp.cumsum(lengths, axis=1)
    starts = ends - lengths
    place = jnp.arange(BIN, dtype=jnp.int32)
    segment = jnp.sum((place[None, :, None] >= ends[:, None, :]).astype(jnp.int32), axis=2)
    opening = jnp.any(
        (place[None, :, None] == starts[:, None, :]) & (lengths[:, None, :] > 0), axis=2
    )
    return segment, opening


ORDERS = {"attn": ("y", "z", "x"), "up": ("z", "x", "y"), "down": ("x", "y", "z")}


def local(hidden_in, token_ids, lengths, owners, w_query, w_key, w_value, w_out, w_up, w_down, gains):
    x_lo, x_hi, core = lax.axis_index("x_lo"), lax.axis_index("x_hi"), lax.axis_index("core")
    place = {"x": x_hi * 2 + x_lo, "y": lax.axis_index("y"), "z": lax.axis_index("z")}
    tables = {name: block_table(order, place, core) for name, order in ORDERS.items()}

    packed = pl.pallas_call(
        pack_kernel,
        out_shape=[pltpu.VMEM((2, 32, D), jnp.bfloat16)] * 3,
        in_specs=[VMEM] * 6,
        out_specs=[VMEM] * 3,
        name="pack",
    )(w_query, w_key, w_value, jnp.swapaxes(w_out, 1, 2), w_up, jnp.swapaxes(w_down, 1, 2))
    names = ("attn", "up", "down")
    blocks = [dict(zip(names, of)) for of in spread(packed, [ORDERS[name] for name in names])]

    segments, openings = passage_tables(lengths)
    segment = lax.dynamic_slice_in_dim(segments, x_lo, 1, 0)
    opening = lax.dynamic_slice_in_dim(openings, x_lo, 1, 0)
    ids = lax.dynamic_slice_in_dim(token_ids.reshape(2, BIN), x_lo, 1, 0)
    seg_col = segment.reshape(BIN, 1)
    keep = (ids >= SKIP_IDS) | opening
    member = (segment == jnp.arange(8, dtype=jnp.int32)[:, None]) & keep
    counts = jnp.sum(member.astype(jnp.float32), axis=1, keepdims=True)
    counts = jnp.where(counts > 0, counts, 1.0)
    member = member.astype(jnp.bfloat16)
    live = lengths.reshape(16) > 0
    owner = owners.reshape(16)
    order = jnp.arange(16, dtype=jnp.int32)
    earlier = (owner[None, :] == owner[:, None]) & live[None, :] & (order[None, :] < order[:, None])
    rank = jnp.sum(earlier.astype(jnp.int32), axis=1)
    target = jnp.where(live, rank * 32 + owner, -1)
    target = lax.dynamic_slice_in_dim(target, x_lo * 8, 8, 0)
    rows = jnp.arange(64, dtype=jnp.int32)
    placing = (rows[:, None] == target[None, :]).astype(jnp.bfloat16).reshape(2, 32, 8)

    hidden = lax.dynamic_slice_in_dim(hidden_in, x_lo * BIN, BIN, 0)
    hidden, tables, gains, seg_col, segment, member, counts, placing, core = lax.optimization_barrier(
        (hidden, tables, gains, seg_col, segment, member, counts, placing, core.reshape(1))
    )
    base = own = other = hidden
    row = pltpu.VMEM((BIN, D), jnp.bfloat16)
    for layer in range(2):
        fresh = layer == 0
        spec, hold = (HBM, in_hbm) if fresh else (VMEM, in_vmem)
        sems = [pltpu.SemaphoreType.DMA((2,))] if fresh else []
        gain = gains[layer - 1, 1][None] if layer else gains[0, 0][None]
        result = pl.pallas_call(
            functools.partial(attention_kernel, layer),
            out_shape=[row] if fresh else [row, row],
            in_specs=[SMEM] + [VMEM] * 6 + [spec] * 4,
            out_specs=[VMEM] if fresh else [VMEM, VMEM],
            scratch_shapes=[
                pltpu.VMEM((2, 32, 32, 1024), jnp.bfloat16),
                pltpu.VMEM((BIN, BIN), jnp.float32),
            ] + sems,
            compiler_params=params(16),
            cost_estimate=pl.CostEstimate(
                flops=0, bytes_accessed=0, transcendentals=0
            ),
            name="attention",
        )(tables["attn"], seg_col, segment, in_vmem(base), in_vmem(own), in_vmem(other), gain, *map(hold, blocks[layer]["attn"]))
        if not fresh:
            hidden = result[0]
        own = result[-1]
        other = swap(own)
        mixed, own = pl.pallas_call(
            functools.partial(ffn_kernel, layer),
            out_shape=[row, row],
            in_specs=[SMEM] * 2 + [VMEM] * 4 + [spec] * 8,
            out_specs=[VMEM, VMEM],
            scratch_shapes=[
                pltpu.VMEM((2, 32, 32, 1024), jnp.bfloat16),
                pltpu.VMEM((2, 32, 32, 1024), jnp.bfloat16),
                pltpu.VMEM((BIN, D), jnp.float32),
                pltpu.VMEM((BIN, D), jnp.bfloat16),
            ] + sems * 2,
            compiler_params=params(16),
            cost_estimate=pl.CostEstimate(
                flops=0, bytes_accessed=0, transcendentals=0
            ),
            name="ffn",
        )(tables["up"], tables["down"], in_vmem(hidden), in_vmem(own), in_vmem(other), gains[layer, 0][None],
          *map(hold, blocks[layer]["up"] + blocks[layer]["down"]))
        other = swap(own)
        base = mixed

    sent = pl.pallas_call(
        pool_kernel,
        out_shape=shape((2, 32, 2, 256)),
        in_specs=[SMEM] + [VMEM] * 7,
        out_specs=VMEM,
        scratch_shapes=[pltpu.VMEM((4, 8, 256), jnp.bfloat16)],
        compiler_params=params(16),
        name="pool",
    )(core, member, counts, placing, in_vmem(base), in_vmem(own), in_vmem(other), gains[1, 1][None])

    names = ("x_lo", "x_hi", "z", "y")
    got = lax.all_to_all(sent.reshape(64, 2, 256), names, split_axis=0, concat_axis=0, tiled=True)
    got = got.reshape(2, 1, 32, 2, 256)
    return got[0] + got[1]


def solution(mesh):
    fine = Mesh(mesh.devices.reshape(2, 2, 2, 4, 4), ("x_lo", "core", "x_hi", "z", "y"))
    encode = ("x_hi", "z", "y")
    trainer = ("x_lo", "core")
    in_specs = (
        P(encode, None),
        P(encode),
        P(encode, None),
        P(encode, None),
        P(None, encode, trainer),
        P(None, encode, trainer),
        P(None, encode, trainer),
        P(None, trainer, encode),
        P(None, encode, trainer),
        P(None, trainer, encode),
        P(),
    )
    out_specs = P(encode, None, None, trainer)
    return jax.shard_map(local, mesh=fine, in_specs=in_specs, out_specs=out_specs, check_vma=False)
```

```python
import functools

import jax
import jax.numpy as jnp
from jax import lax
from jax.experimental import pallas as pl
from jax.experimental.pallas import tpu as pltpu
from jax.sharding import Mesh, PartitionSpec as P

SKIP_IDS = 2000
EPSILON = 1e-05
LOG2E = 1.4426950408889634
HEAD = 64
BIN = 512
D = 1024
RING = 4
NT = (((1,), (1,)), ((), ()))


def x_line(x, core):
    return ((x % 2) * 2 + core) * 2 + x // 2


def hop(value, axis, way=1):
    pairs = []
    for core in range(2):
        step = way if core == 0 else -way
        for at in range(RING):
            to = (at + step) % RING
            if axis == "x":
                pairs.append((x_line(at, core), x_line(to, core)))
            else:
                pairs.append((core * RING + at, core * RING + to))
    names = ("x_lo", "core", "x_hi") if axis == "x" else ("core", axis)
    return lax.ppermute(value, names, pairs)


def swap(value):
    return lax.ppermute(value, "core", [(0, 1), (1, 0)])


def ring(value, axis):
    blocks = [value]
    for _ in range(RING - 1):
        blocks.append(hop(blocks[-1], axis))
    return blocks


def join_kernel(*refs):
    for part in range(3):
        for step in range(RING):
            refs[3 * RING + part][:, step] = refs[part * RING + step][...]


def join(rings):
    flat = [in_vmem(block) for blocks in rings for block in blocks]
    return pl.pallas_call(
        join_kernel,
        out_shape=[pltpu.VMEM((2, RING, 32, D), jnp.bfloat16)] * 3,
        in_specs=[VMEM] * 12,
        out_specs=[VMEM] * 3,
        compiler_params=params(16),
        name="join",
    )(*flat)


def part_kernel(steps, *refs):
    outs = refs[-7:-1]
    copies = []
    for part in range(3):
        for k, step in enumerate(steps):
            source = refs[part * len(steps) + k]
            for layer in range(2):
                target, sem = outs[layer * 3 + part].at[step], refs[-1].at[layer, part, k]
                copies.append(pltpu.make_async_copy(source.at[layer], target, sem))
                copies[-1].start()
    for copy in copies:
        copy.wait()


def part_join(rings, steps, whole=()):
    flat = [in_vmem(blocks[step]) for blocks in rings for step in steps]
    return pl.pallas_call(
        functools.partial(part_kernel, steps),
        out_shape=[pltpu.HBM((RING, RING, 32, D), jnp.bfloat16)] * 6,
        in_specs=[VMEM] * len(flat) + [HBM] * len(whole),
        out_specs=[HBM] * 6,
        input_output_aliases={len(flat) + k: k for k in range(len(whole))},
        scratch_shapes=[pltpu.SemaphoreType.DMA((2, 3, len(steps)))],
        compiler_params=params(16),
        name="join",
    )(*flat, *[in_hbm(value) for value in whole])


def rings(values, axes, short=False):
    one = [hop(value, axis) for value, axis in zip(values, axes)]
    two = [hop(value, axis) for value, axis in zip(one, axes)]
    if short:
        three = [hop(value, axis, -1) for value, axis in zip(values, axes)]
    else:
        three = [hop(value, axis) for value, axis in zip(two, axes)]
    return [list(blocks) for blocks in zip(values, one, two, three)]


def spread(parts, orders):
    axes = [[order[k] for order in orders] for k in range(3)]
    second = rings(join(rings(parts, axes[0], True)), axes[1], True)
    whole = part_join(second, (2,), part_join(second, (0, 1, 3)))
    whole = [value.reshape(RING * RING, 32, D) for value in whole]
    later = rings(whole[3:], axes[2])
    third = []
    for k, (value, axis) in enumerate(zip(whole[:3], axes[2])):
        one = hop(value, axis)
        two = hop(one, axis)
        last = two
        if k == 2:
            last, _ = lax.optimization_barrier((two, later[1][1]))
        third.append([value, one, two, hop(last, axis)])
    return [third, later]


def block_table(order, place, core):
    sign = 1 - 2 * core
    steps = jnp.arange(RING, dtype=jnp.int32)
    at = {}
    for axis, way, dims in zip(order, (sign, sign, sign), ((1, 1, RING), (1, RING, 1), (RING, 1, 1))):
        at[axis] = jnp.mod(place[axis] - way * steps + RING, RING).reshape(dims)
    table = (at["x"] // 2) * 16 + at["z"] * 4 + at["y"]
    return jnp.broadcast_to(table, (RING, RING, RING)).reshape(RING**3)


def pack_kernel(wq, wk, wv, wo, wu, wd, attn, up, down):
    for layer in range(2):
        attn[layer, :, 0:256] = wq[layer]
        attn[layer, :, 256:512] = wk[layer]
        attn[layer, :, 512:768] = wv[layer]
        attn[layer, :, 768:1024] = wo[layer]
        up[layer] = wu[layer]
        down[layer] = wd[layer]


def normalize(values, gain):
    mean = jnp.mean(values, axis=-1, keepdims=True)
    centered = values - mean
    spread_of = jnp.mean(centered * centered, axis=-1, keepdims=True)
    return centered * lax.rsqrt(spread_of + EPSILON) * gain


def settle(base, own, other, gain):
    total = own[...].astype(jnp.float32) + other[...].astype(jnp.float32)
    return normalize(base[...].astype(jnp.float32) + total, gain[...]).astype(jnp.bfloat16)


def indices(order, half):
    spans = [range(RING)] * 3
    spans[order.index("x")] = range(half, RING, 2)
    return [(t, s * RING + f) for t in spans[2] for s in spans[1] for f in spans[0]]


def fetch(order, half, table, blocks, store, sems):
    for third, index in indices(order, half):
        to = table[third * RING * RING + index]
        pltpu.make_async_copy(blocks[third].at[index], store.at[half, to], sems.at[half]).start()


def place(order, half, table, blocks, store, sems):
    if sems is None:
        for third, index in indices(order, half):
            store[half, table[third * RING * RING + index]] = blocks[third][index]
    else:
        pltpu.make_async_copy(store.at[half], store.at[half], sems.at[half]).wait()
    return store[half].reshape(D, D)


def attention_kernel(layer, table, seg_col, seg_row, base, own, other, gain, *rest):
    fresh = layer == 0
    blocks, rest = rest[:4], rest[4:]
    if fresh:
        term, store, bias, sems = rest
        for half in range(2):
            fetch(ORDERS["attn"], half, table, blocks, store, sems)
    else:
        hidden_out, term, store, bias = rest
        sems = None
    bias[...] = jnp.where(seg_col[...] == seg_row[...], 0.0, -1e30)
    if fresh:
        hidden = base[...]
    else:
        hidden = settle(base, own, other, gain)
        hidden_out[...] = hidden
    lane = lax.broadcasted_iota(jnp.int32, (1, 128), 1)
    ones = jnp.ones((BIN, 128), jnp.bfloat16)
    total = None
    for half in range(2):
        weights = place(ORDERS["attn"], half, table, blocks, store, sems)
        qkv = jnp.dot(hidden, weights[:, :768], preferred_element_type=jnp.float32)
        qkv = qkv.astype(jnp.bfloat16)
        contexts = []
        for pair in range(2):
            query = qkv[:, pair * 128 : pair * 128 + 128]
            keys = qkv[:, 256 + pair * 128 : 256 + pair * 128 + 128]
            values = qkv[:, 512 + pair * 128 : 512 + pair * 128 + 128]
            values = jnp.concatenate([values, ones], axis=1)
            rows = []
            for part in range(2):
                span = slice(part * 256, part * 256 + 256)
                both = []
                for head in range(2):
                    mine = (lane < HEAD) if head == 0 else (lane >= HEAD)
                    one = jnp.where(mine, query[span], jnp.zeros((), jnp.bfloat16))
                    scores = lax.dot_general(one, keys, NT, preferred_element_type=jnp.float32)
                    scores = scores + bias[span, :]
                    highest = jnp.max(scores, axis=-1, keepdims=True)
                    probs = jnp.exp2((scores - highest) * (LOG2E * HEAD**-0.5))
                    mixed = jnp.dot(
                        probs.astype(jnp.bfloat16), values, preferred_element_type=jnp.float32
                    )
                    both.append(mixed[:, :128] / mixed[:, 128:])
                rows.append(jnp.where(lane < HEAD, both[0], both[1]).astype(jnp.bfloat16))
            contexts.append(jnp.concatenate(rows, axis=0))
        context = jnp.concatenate(contexts, axis=1)
        piece = lax.dot_general(context, weights[:, 768:], NT, preferred_element_type=jnp.float32)
        total = piece if total is None else total + piece
    term[...] = total.astype(jnp.bfloat16)


def gelu(values):
    return 0.5 * values * (1.0 + lax.erf(values * (0.5**0.5)))


def ffn_kernel(layer, table_up, table_down, base, own, other, gain, *rest):
    up_blocks, down_blocks, rest = rest[:4], rest[4:8], rest[8:]
    mixed_out, term, up_store, down_store, total, active, *sems = rest
    up_sems, down_sems = sems or (None, None)
    if sems:
        for half in range(2):
            fetch(ORDERS["up"], half, table_up, up_blocks, up_store, up_sems)
            fetch(ORDERS["down"], half, table_down, down_blocks, down_store, down_sems)
    mixed = settle(base, own, other, gain)
    mixed_out[...] = mixed
    width = 512
    for half in range(2):
        up = place(ORDERS["up"], half, table_up, up_blocks, up_store, up_sems)
        for cut in range(D // width):
            span = slice(cut * width, cut * width + width)
            raised = jnp.dot(mixed, up[:, span], preferred_element_type=jnp.float32)
            active[:, span] = gelu(raised).astype(jnp.bfloat16)
        down = place(ORDERS["down"], half, table_down, down_blocks, down_store, down_sems)
        for cut in range(D // width):
            span = slice(cut * width, cut * width + width)
            piece = lax.dot_general(active[...], down[span, :], NT, preferred_element_type=jnp.float32)
            if half == 0:
                total[:, span] = piece
            else:
                term[:, span] = (total[:, span] + piece).astype(jnp.bfloat16)


def pool_kernel(core, member, counts, placing, base, own, other, gain, out, store):
    hidden = settle(base, own, other, gain)
    sums = jnp.dot(member[...], hidden, preferred_element_type=jnp.float32)
    pooled = (sums / counts[...]).astype(jnp.bfloat16)
    for piece in range(4):
        store[piece] = pooled[:, piece * 256 : piece * 256 + 256]
    for column in range(2):
        mine = store[column * 2 + core[0]]
        for rank in range(2):
            rows = jnp.dot(placing[rank], mine, preferred_element_type=jnp.float32)
            out[column, :, rank * 2 : rank * 2 + 2, :] = rows.astype(jnp.bfloat16).reshape(32, 2, 128)


def shape(dims, kind=jnp.bfloat16):
    return jax.ShapeDtypeStruct(dims, kind)


VMEM = pl.BlockSpec(memory_space=pltpu.VMEM)
HBM = pl.BlockSpec(memory_space=pltpu.HBM)
SMEM = pl.BlockSpec(memory_space=pltpu.SMEM)


def in_hbm(value):
    return pltpu.with_memory_space_constraint(value, pltpu.HBM)


def in_vmem(value):
    return pltpu.with_memory_space_constraint(value, pltpu.VMEM)


def params(mib):
    return pltpu.CompilerParams(vmem_limit_bytes=mib * 2**20)


def passage_tables(lengths):
    ends = jnp.cumsum(lengths, axis=1)
    starts = ends - lengths
    place = jnp.arange(BIN, dtype=jnp.int32)
    segment = jnp.sum((place[None, :, None] >= ends[:, None, :]).astype(jnp.int32), axis=2)
    opening = jnp.any(
        (place[None, :, None] == starts[:, None, :]) & (lengths[:, None, :] > 0), axis=2
    )
    return segment, opening


ORDERS = {"attn": ("y", "z", "x"), "up": ("z", "x", "y"), "down": ("x", "y", "z")}


def local(hidden_in, token_ids, lengths, owners, w_query, w_key, w_value, w_out, w_up, w_down, gains):
    x_lo, x_hi, core = lax.axis_index("x_lo"), lax.axis_index("x_hi"), lax.axis_index("core")
    place = {"x": x_hi * 2 + x_lo, "y": lax.axis_index("y"), "z": lax.axis_index("z")}
    tables = {name: block_table(order, place, core) for name, order in ORDERS.items()}

    packed = pl.pallas_call(
        pack_kernel,
        out_shape=[pltpu.VMEM((2, 32, D), jnp.bfloat16)] * 3,
        in_specs=[VMEM] * 6,
        out_specs=[VMEM] * 3,
        name="pack",
    )(w_query, w_key, w_value, jnp.swapaxes(w_out, 1, 2), w_up, jnp.swapaxes(w_down, 1, 2))
    names = ("attn", "up", "down")
    blocks = [dict(zip(names, of)) for of in spread(packed, [ORDERS[name] for name in names])]

    segments, openings = passage_tables(lengths)
    segment = lax.dynamic_slice_in_dim(segments, x_lo, 1, 0)
    opening = lax.dynamic_slice_in_dim(openings, x_lo, 1, 0)
    ids = lax.dynamic_slice_in_dim(token_ids.reshape(2, BIN), x_lo, 1, 0)
    seg_col = segment.reshape(BIN, 1)
    keep = (ids >= SKIP_IDS) | opening
    member = (segment == jnp.arange(8, dtype=jnp.int32)[:, None]) & keep
    counts = jnp.sum(member.astype(jnp.float32), axis=1, keepdims=True)
    counts = jnp.where(counts > 0, counts, 1.0)
    member = member.astype(jnp.bfloat16)
    live = lengths.reshape(16) > 0
    owner = owners.reshape(16)
    order = jnp.arange(16, dtype=jnp.int32)
    earlier = (owner[None, :] == owner[:, None]) & live[None, :] & (order[None, :] < order[:, None])
    rank = jnp.sum(earlier.astype(jnp.int32), axis=1)
    target = jnp.where(live, rank * 32 + owner, -1)
    target = lax.dynamic_slice_in_dim(target, x_lo * 8, 8, 0)
    rows = jnp.arange(64, dtype=jnp.int32)
    placing = (rows[:, None] == target[None, :]).astype(jnp.bfloat16).reshape(2, 32, 8)

    hidden = lax.dynamic_slice_in_dim(hidden_in, x_lo * BIN, BIN, 0)
    hidden, tables, gains, seg_col, segment, member, counts, placing, core = lax.optimization_barrier(
        (hidden, tables, gains, seg_col, segment, member, counts, placing, core.reshape(1))
    )
    base = own = other = hidden
    row = pltpu.VMEM((BIN, D), jnp.bfloat16)
    for layer in range(2):
        fresh = layer == 0
        spec, hold = (HBM, in_hbm) if fresh else (VMEM, in_vmem)
        sems = [pltpu.SemaphoreType.DMA((2,))] if fresh else []
        gain = gains[layer - 1, 1][None] if layer else gains[0, 0][None]
        result = pl.pallas_call(
            functools.partial(attention_kernel, layer),
            out_shape=[row] if fresh else [row, row],
            in_specs=[SMEM] + [VMEM] * 6 + [spec] * 4,
            out_specs=[VMEM] if fresh else [VMEM, VMEM],
            scratch_shapes=[
                pltpu.VMEM((2, 32, 32, 1024), jnp.bfloat16),
                pltpu.VMEM((BIN, BIN), jnp.float32),
            ] + sems,
            compiler_params=params(16),
            cost_estimate=pl.CostEstimate(
                flops=0, bytes_accessed=0, transcendentals=0
            ),
            name="attention",
        )(tables["attn"], seg_col, segment, in_vmem(base), in_vmem(own), in_vmem(other), gain, *map(hold, blocks[layer]["attn"]))
        if not fresh:
            hidden = result[0]
        own = result[-1]
        other = swap(own)
        if fresh:
            group = blocks[1]["attn"]
            value, _ = lax.optimization_barrier((group[0], group[1]))
            blocks[1]["attn"] = group[:3] + [hop(value, "x", -1)]
        mixed, own = pl.pallas_call(
            functools.partial(ffn_kernel, layer),
            out_shape=[row, row],
            in_specs=[SMEM] * 2 + [VMEM] * 4 + [spec] * 8,
            out_specs=[VMEM, VMEM],
            scratch_shapes=[
                pltpu.VMEM((2, 32, 32, 1024), jnp.bfloat16),
                pltpu.VMEM((2, 32, 32, 1024), jnp.bfloat16),
                pltpu.VMEM((BIN, D), jnp.float32),
                pltpu.VMEM((BIN, D), jnp.bfloat16),
            ] + sems * 2,
            compiler_params=params(16),
            cost_estimate=pl.CostEstimate(
                flops=0, bytes_accessed=0, transcendentals=0
            ),
            name="ffn",
        )(tables["up"], tables["down"], in_vmem(hidden), in_vmem(own), in_vmem(other), gains[layer, 0][None],
          *map(hold, blocks[layer]["up"] + blocks[layer]["down"]))
        other = swap(own)
        base = mixed

    sent = pl.pallas_call(
        pool_kernel,
        out_shape=shape((2, 32, 4, 128)),
        in_specs=[SMEM] + [VMEM] * 7,
        out_specs=VMEM,
        scratch_shapes=[pltpu.VMEM((4, 8, 256), jnp.bfloat16)],
        compiler_params=params(16),
        name="pool",
    )(core, member, counts, placing, in_vmem(base), in_vmem(own), in_vmem(other), gains[1, 1][None])

    names = ("x_lo", "x_hi", "z", "y")
    got = lax.all_to_all(sent.reshape(64, 4, 128), names, split_axis=0, concat_axis=0, tiled=True)
    got = got.reshape(2, 1, 32, 2, 256)
    return got[0] + got[1]


def solution(mesh):
    fine = Mesh(mesh.devices.reshape(2, 2, 2, 4, 4), ("x_lo", "core", "x_hi", "z", "y"))
    encode = ("x_hi", "z", "y")
    trainer = ("x_lo", "core")
    in_specs = (
        P(encode, None),
        P(encode),
        P(encode, None),
        P(encode, None),
        P(None, encode, trainer),
        P(None, encode, trainer),
        P(None, encode, trainer),
        P(None, trainer, encode),
        P(None, encode, trainer),
        P(None, trainer, encode),
        P(),
    )
    out_specs = P(encode, None, None, trainer)
    return jax.shard_map(local, mesh=fine, in_specs=in_specs, out_specs=out_specs, check_vma=False)
```

```python
import functools

import jax
import jax.numpy as jnp
from jax import lax
from jax.experimental import pallas as pl
from jax.experimental.pallas import tpu as pltpu
from jax.sharding import Mesh, PartitionSpec as P

SKIP_IDS = 2000
EPSILON = 1e-05
LOG2E = 1.4426950408889634
HEAD = 64
BIN = 512
D = 1024
RING = 4
NT = (((1,), (1,)), ((), ()))


def x_line(x, core):
    return ((x % 2) * 2 + core) * 2 + x // 2


def hop(value, axis, way=1):
    pairs = []
    for core in range(2):
        step = way if core == 0 else -way
        for at in range(RING):
            to = (at + step) % RING
            if axis == "x":
                pairs.append((x_line(at, core), x_line(to, core)))
            else:
                pairs.append((core * RING + at, core * RING + to))
    names = ("x_lo", "core", "x_hi") if axis == "x" else ("core", axis)
    return lax.ppermute(value, names, pairs)


def swap(value):
    return lax.ppermute(value, "core", [(0, 1), (1, 0)])


def ring(value, axis):
    blocks = [value]
    for _ in range(RING - 1):
        blocks.append(hop(blocks[-1], axis))
    return blocks


def join_kernel(*refs):
    for part in range(3):
        for step in range(RING):
            refs[3 * RING + part][:, step] = refs[part * RING + step][...]


def join(rings):
    flat = [in_vmem(block) for blocks in rings for block in blocks]
    return pl.pallas_call(
        join_kernel,
        out_shape=[pltpu.VMEM((2, RING, 32, D), jnp.bfloat16)] * 3,
        in_specs=[VMEM] * 12,
        out_specs=[VMEM] * 3,
        compiler_params=params(16),
        name="join",
    )(*flat)


def part_kernel(steps, *refs):
    outs = refs[-7:-1]
    copies = []
    for part in range(3):
        for k, step in enumerate(steps):
            source = refs[part * len(steps) + k]
            for layer in range(2):
                target, sem = outs[layer * 3 + part].at[step], refs[-1].at[layer, part, k]
                copies.append(pltpu.make_async_copy(source.at[layer], target, sem))
                copies[-1].start()
    for copy in copies:
        copy.wait()


def part_join(rings, steps, whole=()):
    flat = [in_vmem(blocks[step]) for blocks in rings for step in steps]
    return pl.pallas_call(
        functools.partial(part_kernel, steps),
        out_shape=[pltpu.HBM((RING, RING, 32, D), jnp.bfloat16)] * 6,
        in_specs=[VMEM] * len(flat) + [HBM] * len(whole),
        out_specs=[HBM] * 6,
        input_output_aliases={len(flat) + k: k for k in range(len(whole))},
        scratch_shapes=[pltpu.SemaphoreType.DMA((2, 3, len(steps)))],
        compiler_params=params(16),
        name="join",
    )(*flat, *[in_hbm(value) for value in whole])


def rings(values, axes, short=False):
    one = [hop(value, axis) for value, axis in zip(values, axes)]
    two = [hop(value, axis) for value, axis in zip(one, axes)]
    if short:
        three = [hop(value, axis, -1) for value, axis in zip(values, axes)]
    else:
        three = [hop(value, axis) for value, axis in zip(two, axes)]
    return [list(blocks) for blocks in zip(values, one, two, three)]


def spread(parts, orders):
    axes = [[order[k] for order in orders] for k in range(3)]
    second = rings(join(rings(parts, axes[0], True)), axes[1], True)
    whole = part_join(second, (2,), part_join(second, (0, 1, 3)))
    whole = [value.reshape(RING * RING, 32, D) for value in whole]
    return [rings(whole[3 * layer : 3 * layer + 3], axes[2]) for layer in range(2)]


def block_table(order, place, core):
    sign = 1 - 2 * core
    steps = jnp.arange(RING, dtype=jnp.int32)
    at = {}
    for axis, way, dims in zip(order, (sign, sign, sign), ((1, 1, RING), (1, RING, 1), (RING, 1, 1))):
        at[axis] = jnp.mod(place[axis] - way * steps + RING, RING).reshape(dims)
    table = (at["x"] // 2) * 16 + at["z"] * 4 + at["y"]
    return jnp.broadcast_to(table, (RING, RING, RING)).reshape(RING**3)


def pack_kernel(wq, wk, wv, wo, wu, wd, attn, up, down):
    for layer in range(2):
        attn[layer, :, 0:256] = wq[layer]
        attn[layer, :, 256:512] = wk[layer]
        attn[layer, :, 512:768] = wv[layer]
        attn[layer, :, 768:1024] = wo[layer]
        up[layer] = wu[layer]
        down[layer] = wd[layer]


def normalize(values, gain):
    mean = jnp.mean(values, axis=-1, keepdims=True)
    centered = values - mean
    spread_of = jnp.mean(centered * centered, axis=-1, keepdims=True)
    return centered * lax.rsqrt(spread_of + EPSILON) * gain


def settle(base, own, other, gain):
    total = own[...].astype(jnp.float32) + other[...].astype(jnp.float32)
    return normalize(base[...].astype(jnp.float32) + total, gain[...]).astype(jnp.bfloat16)


def indices(order, half):
    spans = [range(RING)] * 3
    spans[order.index("x")] = range(half, RING, 2)
    return [(t, s * RING + f) for t in spans[2] for s in spans[1] for f in spans[0]]


def fetch(order, half, table, blocks, store, sems):
    for third, index in indices(order, half):
        to = table[third * RING * RING + index]
        pltpu.make_async_copy(blocks[third].at[index], store.at[half, to], sems.at[half]).start()


def place(order, half, table, blocks, store, sems):
    if sems is None:
        for third, index in indices(order, half):
            store[half, table[third * RING * RING + index]] = blocks[third][index]
    else:
        pltpu.make_async_copy(store.at[half], store.at[half], sems.at[half]).wait()
    return store[half].reshape(D, D)


def attention_kernel(layer, table, seg_col, seg_row, base, own, other, gain, *rest):
    fresh = layer == 0
    blocks, rest = rest[:4], rest[4:]
    if fresh:
        term, store, bias, sems = rest
        for half in range(2):
            fetch(ORDERS["attn"], half, table, blocks, store, sems)
    else:
        hidden_out, term, store, bias = rest
        sems = None
    bias[...] = jnp.where(seg_col[...] == seg_row[...], 0.0, -1e30)
    if fresh:
        hidden = base[...]
    else:
        hidden = settle(base, own, other, gain)
        hidden_out[...] = hidden
    lane = lax.broadcasted_iota(jnp.int32, (1, 128), 1)
    ones = jnp.ones((BIN, 128), jnp.bfloat16)
    total = None
    for half in range(2):
        weights = place(ORDERS["attn"], half, table, blocks, store, sems)
        qkv = jnp.dot(hidden, weights[:, :768], preferred_element_type=jnp.float32)
        qkv = qkv.astype(jnp.bfloat16)
        contexts = []
        for pair in range(2):
            query = qkv[:, pair * 128 : pair * 128 + 128]
            keys = qkv[:, 256 + pair * 128 : 256 + pair * 128 + 128]
            values = qkv[:, 512 + pair * 128 : 512 + pair * 128 + 128]
            values = jnp.concatenate([values, ones], axis=1)
            rows = []
            for part in range(2):
                span = slice(part * 256, part * 256 + 256)
                both = []
                for head in range(2):
                    mine = (lane < HEAD) if head == 0 else (lane >= HEAD)
                    one = jnp.where(mine, query[span], jnp.zeros((), jnp.bfloat16))
                    scores = lax.dot_general(one, keys, NT, preferred_element_type=jnp.float32)
                    scores = scores + bias[span, :]
                    highest = jnp.max(scores, axis=-1, keepdims=True)
                    probs = jnp.exp2((scores - highest) * (LOG2E * HEAD**-0.5))
                    mixed = jnp.dot(
                        probs.astype(jnp.bfloat16), values, preferred_element_type=jnp.float32
                    )
                    both.append(mixed[:, :128] / mixed[:, 128:])
                rows.append(jnp.where(lane < HEAD, both[0], both[1]).astype(jnp.bfloat16))
            contexts.append(jnp.concatenate(rows, axis=0))
        context = jnp.concatenate(contexts, axis=1)
        piece = lax.dot_general(context, weights[:, 768:], NT, preferred_element_type=jnp.float32)
        total = piece if total is None else total + piece
    term[...] = total.astype(jnp.bfloat16)


def gelu(values):
    return 0.5 * values * (1.0 + lax.erf(values * (0.5**0.5)))


def ffn_kernel(layer, table_up, table_down, base, own, other, gain, *rest):
    up_blocks, down_blocks, rest = rest[:4], rest[4:8], rest[8:]
    mixed_out, term, up_store, down_store, total, active, *sems = rest
    up_sems, down_sems = sems or (None, None)
    if sems:
        for half in range(2):
            fetch(ORDERS["up"], half, table_up, up_blocks, up_store, up_sems)
            fetch(ORDERS["down"], half, table_down, down_blocks, down_store, down_sems)
    mixed = settle(base, own, other, gain)
    mixed_out[...] = mixed
    width = 512
    for half in range(2):
        up = place(ORDERS["up"], half, table_up, up_blocks, up_store, up_sems)
        for cut in range(D // width):
            span = slice(cut * width, cut * width + width)
            raised = jnp.dot(mixed, up[:, span], preferred_element_type=jnp.float32)
            active[:, span] = gelu(raised).astype(jnp.bfloat16)
        down = place(ORDERS["down"], half, table_down, down_blocks, down_store, down_sems)
        for cut in range(D // width):
            span = slice(cut * width, cut * width + width)
            piece = lax.dot_general(active[...], down[span, :], NT, preferred_element_type=jnp.float32)
            if half == 0:
                total[:, span] = piece
            else:
                term[:, span] = (total[:, span] + piece).astype(jnp.bfloat16)


def pool_kernel(core, member, counts, placing, base, own, other, gain, out, store):
    hidden = settle(base, own, other, gain)
    sums = jnp.dot(member[...], hidden, preferred_element_type=jnp.float32)
    pooled = (sums / counts[...]).astype(jnp.bfloat16)
    for piece in range(4):
        store[piece] = pooled[:, piece * 256 : piece * 256 + 256]
    for column in range(2):
        mine = store[column * 2 + core[0]]
        for rank in range(2):
            rows = jnp.dot(placing[rank], mine, preferred_element_type=jnp.float32)
            out[column, :, rank * 2 : rank * 2 + 2, :] = rows.astype(jnp.bfloat16).reshape(32, 2, 128)


def shape(dims, kind=jnp.bfloat16):
    return jax.ShapeDtypeStruct(dims, kind)


VMEM = pl.BlockSpec(memory_space=pltpu.VMEM)
HBM = pl.BlockSpec(memory_space=pltpu.HBM)
SMEM = pl.BlockSpec(memory_space=pltpu.SMEM)


def in_hbm(value):
    return pltpu.with_memory_space_constraint(value, pltpu.HBM)


def in_vmem(value):
    return pltpu.with_memory_space_constraint(value, pltpu.VMEM)


def params(mib):
    return pltpu.CompilerParams(vmem_limit_bytes=mib * 2**20)


def passage_tables(lengths):
    ends = jnp.cumsum(lengths, axis=1)
    starts = ends - lengths
    place = jnp.arange(BIN, dtype=jnp.int32)
    segment = jnp.sum((place[None, :, None] >= ends[:, None, :]).astype(jnp.int32), axis=2)
    opening = jnp.any(
        (place[None, :, None] == starts[:, None, :]) & (lengths[:, None, :] > 0), axis=2
    )
    return segment, opening


ORDERS = {"attn": ("y", "z", "x"), "up": ("z", "x", "y"), "down": ("x", "y", "z")}


def local(hidden_in, token_ids, lengths, owners, w_query, w_key, w_value, w_out, w_up, w_down, gains):
    x_lo, x_hi, core = lax.axis_index("x_lo"), lax.axis_index("x_hi"), lax.axis_index("core")
    place = {"x": x_hi * 2 + x_lo, "y": lax.axis_index("y"), "z": lax.axis_index("z")}
    tables = {name: block_table(order, place, core) for name, order in ORDERS.items()}

    packed = pl.pallas_call(
        pack_kernel,
        out_shape=[pltpu.VMEM((2, 32, D), jnp.bfloat16)] * 3,
        in_specs=[VMEM] * 6,
        out_specs=[VMEM] * 3,
        name="pack",
    )(w_query, w_key, w_value, jnp.swapaxes(w_out, 1, 2), w_up, jnp.swapaxes(w_down, 1, 2))
    names = ("attn", "up", "down")
    blocks = [dict(zip(names, of)) for of in spread(packed, [ORDERS[name] for name in names])]

    segments, openings = passage_tables(lengths)
    segment = lax.dynamic_slice_in_dim(segments, x_lo, 1, 0)
    opening = lax.dynamic_slice_in_dim(openings, x_lo, 1, 0)
    ids = lax.dynamic_slice_in_dim(token_ids.reshape(2, BIN), x_lo, 1, 0)
    seg_col = segment.reshape(BIN, 1)
    keep = (ids >= SKIP_IDS) | opening
    member = (segment == jnp.arange(8, dtype=jnp.int32)[:, None]) & keep
    counts = jnp.sum(member.astype(jnp.float32), axis=1, keepdims=True)
    counts = jnp.where(counts > 0, counts, 1.0)
    member = member.astype(jnp.bfloat16)
    live = lengths.reshape(16) > 0
    owner = owners.reshape(16)
    order = jnp.arange(16, dtype=jnp.int32)
    earlier = (owner[None, :] == owner[:, None]) & live[None, :] & (order[None, :] < order[:, None])
    rank = jnp.sum(earlier.astype(jnp.int32), axis=1)
    target = jnp.where(live, rank * 32 + owner, -1)
    target = lax.dynamic_slice_in_dim(target, x_lo * 8, 8, 0)
    rows = jnp.arange(64, dtype=jnp.int32)
    placing = (rows[:, None] == target[None, :]).astype(jnp.bfloat16).reshape(2, 32, 8)

    hidden = lax.dynamic_slice_in_dim(hidden_in, x_lo * BIN, BIN, 0)
    hidden, tables, gains, seg_col, segment, member, counts, placing, core = lax.optimization_barrier(
        (hidden, tables, gains, seg_col, segment, member, counts, placing, core.reshape(1))
    )
    base = own = other = hidden
    row = pltpu.VMEM((BIN, D), jnp.bfloat16)
    for layer in range(2):
        fresh = layer == 0
        spec, hold = (HBM, in_hbm) if fresh else (VMEM, in_vmem)
        sems = [pltpu.SemaphoreType.DMA((2,))] if fresh else []
        gain = gains[layer - 1, 1][None] if layer else gains[0, 0][None]
        result = pl.pallas_call(
            functools.partial(attention_kernel, layer),
            out_shape=[row] if fresh else [row, row],
            in_specs=[SMEM] + [VMEM] * 6 + [spec] * 4,
            out_specs=[VMEM] if fresh else [VMEM, VMEM],
            scratch_shapes=[
                pltpu.VMEM((2, 32, 32, 1024), jnp.bfloat16),
                pltpu.VMEM((BIN, BIN), jnp.float32),
            ] + sems,
            compiler_params=params(16),
            cost_estimate=pl.CostEstimate(
                flops=0, bytes_accessed=0, transcendentals=0
            ),
            name="attention",
        )(tables["attn"], seg_col, segment, in_vmem(base), in_vmem(own), in_vmem(other), gain, *map(hold, blocks[layer]["attn"]))
        if not fresh:
            hidden = result[0]
        own = result[-1]
        other = swap(own)
        if fresh:
            group = blocks[1]["attn"]
            value, _ = lax.optimization_barrier((group[0], group[1]))
            blocks[1]["attn"] = group[:3] + [hop(value, "x", -1)]
        mixed, own = pl.pallas_call(
            functools.partial(ffn_kernel, layer),
            out_shape=[row, row],
            in_specs=[SMEM] * 2 + [VMEM] * 4 + [spec] * 8,
            out_specs=[VMEM, VMEM],
            scratch_shapes=[
                pltpu.VMEM((2, 32, 32, 1024), jnp.bfloat16),
                pltpu.VMEM((2, 32, 32, 1024), jnp.bfloat16),
                pltpu.VMEM((BIN, D), jnp.float32),
                pltpu.VMEM((BIN, D), jnp.bfloat16),
            ] + sems * 2,
            compiler_params=params(16),
            cost_estimate=pl.CostEstimate(
                flops=0, bytes_accessed=0, transcendentals=0
            ),
            name="ffn",
        )(tables["up"], tables["down"], in_vmem(hidden), in_vmem(own), in_vmem(other), gains[layer, 0][None],
          *map(hold, blocks[layer]["up"] + blocks[layer]["down"]))
        other = swap(own)
        base = mixed

    sent = pl.pallas_call(
        pool_kernel,
        out_shape=shape((2, 32, 4, 128)),
        in_specs=[SMEM] + [VMEM] * 7,
        out_specs=VMEM,
        scratch_shapes=[pltpu.VMEM((4, 8, 256), jnp.bfloat16)],
        compiler_params=params(16),
        name="pool",
    )(core, member, counts, placing, in_vmem(base), in_vmem(own), in_vmem(other), gains[1, 1][None])

    names = ("x_lo", "x_hi", "z", "y")
    got = lax.all_to_all(sent.reshape(64, 4, 128), names, split_axis=0, concat_axis=0, tiled=True)
    got = got.reshape(2, 1, 32, 2, 256)
    return got[0] + got[1]


def solution(mesh):
    fine = Mesh(mesh.devices.reshape(2, 2, 2, 4, 4), ("x_lo", "core", "x_hi", "z", "y"))
    encode = ("x_hi", "z", "y")
    trainer = ("x_lo", "core")
    in_specs = (
        P(encode, None),
        P(encode),
        P(encode, None),
        P(encode, None),
        P(None, encode, trainer),
        P(None, encode, trainer),
        P(None, encode, trainer),
        P(None, trainer, encode),
        P(None, encode, trainer),
        P(None, trainer, encode),
        P(),
    )
    out_specs = P(encode, None, None, trainer)
    return jax.shard_map(local, mesh=fine, in_specs=in_specs, out_specs=out_specs, check_vma=False)
```
